512 devices in a mesh: seq: 128 (over z, y, core), spill: 4 (over x).
Axes of the slice: x: 4, y: 8, z: 8, core: 2. Of those that a mesh axis runs over, the one named last changes fastest.
Arguments:
- queries: bfloat16 [65536, 1024], P(('seq', 'spill')), may hold values from -192 to 192
- keys: bfloat16 [65536, 1024], P(('seq', 'spill')), may hold values from -6 to 6
- values: bfloat16 [65536, 1024], P(('seq', 'spill')), may hold values from -6 to 6
- out_grad: bfloat16 [65536, 1024], P(('seq', 'spill')), may hold values from -6 to 6
- cluster_ids: int32 [65536, 8], P(('seq', 'spill')), may hold values from 0 to 255, as said below
Outputs:
- query_grad: bfloat16 [65536, 1024], P(('seq', 'spill'))
- key_grad: bfloat16 [65536, 1024], P(('seq', 'spill'))
- value_grad: bfloat16 [65536, 1024], P(('seq', 'spill'))
The draws below stay inside these ranges and needn't reach their ends.
Inputs may be any that keep to these rules, and one draw needn't show every extreme that they name: `cluster_ids`: cluster c belongs to owner c % 128. In every aligned block of 128 rows and every head, at most 2 rows name clusters of one owner; in every draw some block reaches 2 for some owner, and in one head every block sends 2 rows to one common owner.
All inputs are finite; a program needn't handle non-finite values.
Results may differ from the reference program's by a relative error of at most 0.012.
Values may be sent and summed in bfloat16 or wider, within the bound.
No kernel may reach another device: no remote copies, remote signals or barrier semaphores. Data moves between devices by JAX's collectives and lax.ppermute only.
A program may use at most 64 MiB of HBM per device.

```python
import jax
import jax.numpy as jnp
from jax import lax

HEADS = 8
HD = 128
CLU_DEV = 2
TOK_DEV = 128
TOKENS = 65536
CLUSTERS = 256
CAP = 2
N_SPILL = 4


def shared_normal(key):
    return jnp.clip(jax.random.normal(key, (TOKENS, HEADS * HD), jnp.float32), -6.0, 6.0)


def draw_keys(key, part):
    base = shared_normal(key)
    return base.astype(jnp.bfloat16)


def draw_queries(key, part):
    key = jax.random.fold_in(key, 7)
    first_key = jax.random.fold_in(key, 0)
    result = jnp.clip(jax.random.normal(first_key, (TOKENS, HEADS * HD), jnp.float32), -6.0, 6.0)
    return result.astype(jnp.bfloat16)


def draw_cluster_ids(key, part):
    key = jax.random.fold_in(key, 11)
    split_keys = jax.random.split(key, 6)
    owner_count = CLUSTERS // CLU_DEV
    block_count = TOKENS // TOK_DEV
    ranking = jax.random.randint(split_keys[0], (block_count, HEADS, TOK_DEV), 0, 1 << 20) * TOK_DEV + jnp.arange(TOK_DEV, dtype=jnp.int32)
    place_in = jnp.argsort(jnp.argsort(ranking, axis=2), axis=2).astype(jnp.int32)
    lowest = max(1, CAP // 2)
    group_sizes = jax.random.randint(split_keys[1], (block_count, HEADS, owner_count), lowest, CAP + 1)
    group_sizes = group_sizes.at[:, :, 0].set(CAP)
    bounds = jnp.cumsum(group_sizes, axis=2)
    group_index = jnp.sum((bounds[:, :, None, :] <= place_in[:, :, :, None]).astype(jnp.int32), axis=3)
    shift_by = jax.random.randint(split_keys[2], (block_count, HEADS, 1), 0, owner_count)
    full_head = jax.random.randint(split_keys[3], (), 0, HEADS)
    full_owner = jax.random.randint(split_keys[4], (), 0, owner_count)
    head_match = (jnp.arange(HEADS, dtype=jnp.int32) == full_head)[None, :, None]
    shift_by = jnp.where(head_match, full_owner, shift_by)
    owner_of = (shift_by + group_index) % owner_count
    inner_cluster = jnp.minimum(jax.random.randint(split_keys[5], (block_count, HEADS, TOK_DEV), 0, 2 * CLU_DEV), CLU_DEV - 1)
    ids_all = owner_of + owner_count * inner_cluster
    return jnp.transpose(ids_all, (0, 2, 1)).reshape(TOKENS, HEADS).astype(jnp.int32)


def block_levels(own_key, dims, cuts, low, high):
    loudness = 1.0
    for axis_at, blocks in cuts:
        heights = jax.random.uniform(jax.random.fold_in(jax.random.fold_in(own_key, 6), axis_at), (blocks,), jnp.float32, low / len(cuts), high / len(cuts))
        loudness = loudness * jnp.repeat(jnp.exp(heights), dims[axis_at] // blocks).reshape((-1,) + (1,) * (len(dims) - 1 - axis_at))
    return loudness


def gaussian(stream_key, shape, scale, most, pieces=(), kind=jnp.bfloat16):
    entries = scale * jax.random.normal(stream_key, shape, jnp.float32)
    if pieces:
        entries = entries * block_levels(stream_key, shape, pieces, -0.22, 0.18)
    return jnp.clip(entries, -most, most).astype(kind)


def setup_inputs(seed: int = 0) -> dict:
    key_of = jax.random.split(jax.random.key(seed), 6)
    queries = draw_queries(jax.random.fold_in(key_of[5], 71), 0)
    keys = draw_keys(jax.random.fold_in(key_of[5], 71), 0)
    values = gaussian(key_of[2], (TOKENS, HEADS * HD), 1.0, 6.0, ((0, 512),))
    out_grad = gaussian(key_of[3], (TOKENS, HEADS * HD), 1.0, 6.0, ((0, 512),))
    cluster_ids = draw_cluster_ids(jax.random.fold_in(key_of[5], 71), 0)
    return {"queries": queries, "keys": keys, "values": values, "out_grad": out_grad, "cluster_ids": cluster_ids}


MASKED_SCORE = -1.0e30


def attend(q_rows, g_rows, q_ids, q_pos, k_rows, v_rows, k_ids, k_pos):
    score_scale = q_rows.shape[1] ** -0.5
    raw_scores = jnp.dot(q_rows, k_rows.T, preferred_element_type=jnp.float32) * score_scale
    allowed = (q_ids[:, None] == k_ids[None, :]) & (k_pos[None, :] <= q_pos[:, None])
    row_max = jnp.max(jnp.where(allowed, raw_scores, MASKED_SCORE), axis=1, keepdims=True)
    weights_raw = jnp.where(allowed, jnp.exp(raw_scores - row_max), 0.0)
    probability = weights_raw / jnp.sum(weights_raw, axis=1, keepdims=True)
    prob_half = probability.astype(jnp.bfloat16)
    attended = jnp.dot(prob_half, v_rows, preferred_element_type=jnp.float32)
    row_delta = jnp.sum(g_rows.astype(jnp.float32) * attended, axis=1, keepdims=True)
    prob_grad = jnp.dot(g_rows, v_rows.T, preferred_element_type=jnp.float32)
    score_grad = (probability * (prob_grad - row_delta) * score_scale).astype(jnp.bfloat16)
    return prob_half, score_grad


def head_grads(per_item):
    q_cols, k_cols, v_cols, g_cols, ids_col = per_item
    tokens_total = ids_col.shape[0]
    block_rows = min(512, tokens_total)
    reach = (tokens_total // TOK_DEV) * CAP
    position = jnp.arange(tokens_total, dtype=jnp.int32)
    order = jnp.argsort(ids_col.astype(jnp.int32) * tokens_total + position).astype(jnp.int32)
    q_sorted = jnp.take(q_cols, order, axis=0)
    k_sorted = jnp.take(k_cols, order, axis=0)
    v_sorted = jnp.take(v_cols, order, axis=0)
    g_sorted = jnp.take(g_cols, order, axis=0)
    id_sorted = jnp.take(ids_col, order, axis=0).astype(jnp.int32)
    pos_sorted = order
    group_sorted = (pos_sorted // TOK_DEV) % N_SPILL
    k_padded = jnp.concatenate([jnp.zeros((reach, HD), k_sorted.dtype), k_sorted], axis=0)
    v_padded = jnp.concatenate([jnp.zeros((reach, HD), v_sorted.dtype), v_sorted], axis=0)
    id_padded = jnp.concatenate([jnp.full((reach,), -1, jnp.int32), id_sorted], axis=0)
    pos_padded = jnp.concatenate([jnp.zeros((reach,), jnp.int32), pos_sorted], axis=0)
    window = reach + block_rows
    group_iota = jnp.arange(N_SPILL, dtype=jnp.int32)

    def step(carry, index):
        key_acc, value_acc = carry
        start = (index * block_rows).astype(jnp.int32)
        q_blk = lax.dynamic_slice_in_dim(q_sorted, start, block_rows, 0)
        g_blk = lax.dynamic_slice_in_dim(g_sorted, start, block_rows, 0)
        qid_blk = lax.dynamic_slice_in_dim(id_sorted, start, block_rows, 0)
        qpos_blk = lax.dynamic_slice_in_dim(pos_sorted, start, block_rows, 0)
        qgrp_blk = lax.dynamic_slice_in_dim(group_sorted, start, block_rows, 0)
        k_win = lax.dynamic_slice_in_dim(k_padded, start, window, 0)
        v_win = lax.dynamic_slice_in_dim(v_padded, start, window, 0)
        kid_win = lax.dynamic_slice_in_dim(id_padded, start, window, 0)
        kpos_win = lax.dynamic_slice_in_dim(pos_padded, start, window, 0)
        prob_half, score_grad = attend(q_blk, g_blk, qid_blk, qpos_blk, k_win, v_win, kid_win, kpos_win)
        query_blk = jnp.dot(score_grad, k_win, preferred_element_type=jnp.float32).astype(jnp.bfloat16)
        group_mask = (qgrp_blk[None, :] == group_iota[:, None]).astype(jnp.float32)
        q_split = q_blk.astype(jnp.float32)[None] * group_mask[:, :, None]
        g_split = g_blk.astype(jnp.float32)[None] * group_mask[:, :, None]
        key_win = jnp.einsum("qk,rqd->rkd", score_grad.astype(jnp.float32), q_split)
        value_win = jnp.einsum("qk,rqd->rkd", prob_half.astype(jnp.float32), g_split)
        key_acc = lax.dynamic_update_slice_in_dim(key_acc, lax.dynamic_slice_in_dim(key_acc, start, window, 1) + key_win, start, 1)
        value_acc = lax.dynamic_update_slice_in_dim(value_acc, lax.dynamic_slice_in_dim(value_acc, start, window, 1) + value_win, start, 1)
        return (key_acc, value_acc), query_blk

    empty_acc = jnp.zeros((N_SPILL, reach + tokens_total, HD), jnp.float32)
    (key_acc, value_acc), query_blocks = lax.scan(step, (empty_acc, empty_acc), jnp.arange(tokens_total // block_rows, dtype=jnp.int32))
    query_sorted = query_blocks.reshape(tokens_total, HD)

    def combine_parts(accum):
        parts = lax.optimization_barrier(accum[:, reach:].astype(jnp.bfloat16))
        return jnp.sum(parts.astype(jnp.float32), axis=0).astype(jnp.bfloat16)

    key_sorted_grad = combine_parts(key_acc)
    value_sorted_grad = combine_parts(value_acc)

    def unsort(sorted_rows):
        return jnp.zeros_like(sorted_rows).at[order].set(sorted_rows)

    return unsort(query_sorted), unsort(key_sorted_grad), unsort(value_sorted_grad)


def reference(queries, keys, values, out_grad, cluster_ids):
    tokens_total = queries.shape[0]

    def by_head(matrix):
        return jnp.transpose(matrix.reshape(tokens_total, HEADS, HD), (1, 0, 2))

    def to_columns(stacked):
        return jnp.transpose(stacked, (1, 0, 2)).reshape(tokens_total, HEADS * HD)

    query_grad, key_grad, value_grad = lax.map(head_grads, (by_head(queries), by_head(keys), by_head(values), by_head(out_grad), jnp.transpose(cluster_ids).astype(jnp.int32)))
    return to_columns(query_grad), to_columns(key_grad), to_columns(value_grad)
```

```python
import functools

import jax
import jax.numpy as jnp
from jax import lax
from jax.experimental import pallas as pl
from jax.experimental.pallas import tpu as pltpu
from jax.sharding import PartitionSpec as P

AXES = ("seq", "spill")
LANES = 128
SLOTS = 2
MASKED_SCORE = -1e30
LOWEST_MAX = -5e29


def dot(left, right):
    return jnp.dot(left, right, preferred_element_type=jnp.float32)


def dot_last(left, right):
    return lax.dot_general(
        left, right, (((1,), (1,)), ((), ())), preferred_element_type=jnp.float32
    )


def iota(rows, columns, axis):
    return lax.broadcasted_iota(jnp.int32, (rows, columns), axis)


def place_kernel(owners, spills, q_ref, k_ref, v_ref, g_ref, ids_ref, out_ref, rows_ref):
    tokens, heads = ids_ref.shape
    per_dest = heads // spills
    arrays = (q_ref, k_ref, v_ref, g_ref)
    data_rows = per_dest * len(arrays) * SLOTS
    message = data_rows + per_dest
    owner_iota = iota(owners, tokens, 0)
    earlier = (iota(tokens, tokens, 0) < iota(tokens, tokens, 1)).astype(jnp.bfloat16)
    first_lanes = iota(owners, LANES, 1) < LANES // 2
    for head in range(heads):
        dest, within = divmod(head, per_dest)
        id_column = ids_ref[:, head : head + 1].astype(jnp.float32)
        ids = jnp.transpose(jnp.broadcast_to(id_column, (tokens, owners))).astype(jnp.int32)
        hot = ids % owners == owner_iota
        count = dot(hot.astype(jnp.bfloat16), earlier)
        first = hot & (count < 0.5)
        second = hot & (count > 0.5)
        select = jnp.concatenate([first.astype(jnp.bfloat16), second.astype(jnp.bfloat16)], axis=0)
        columns = slice(head * LANES, (head + 1) * LANES)
        placed = dot(select, jnp.concatenate([ref[:, columns] for ref in arrays], axis=1))
        base = dest * message
        for array in range(len(arrays)):
            for slot in range(SLOTS):
                row = base + (within * len(arrays) + array) * SLOTS + slot
                rows_ref[pl.ds(row, owners, stride=spills * message), :] = placed[
                    slot * owners : (slot + 1) * owners, array * LANES : (array + 1) * LANES
                ]
        label = (ids // owners + 1).astype(jnp.float32)
        first_label = jnp.sum(jnp.where(first, label, 0.0), axis=1, keepdims=True)
        second_label = jnp.sum(jnp.where(second, label, 0.0), axis=1, keepdims=True)
        rows_ref[pl.ds(base + data_rows + within, owners, stride=spills * message), :] = jnp.where(
            first_lanes, first_label, second_label
        )
    out_ref[...] = rows_ref[...].astype(jnp.bfloat16)


def attend_kernel(per_dest, message, x_ref, out_ref, rows_ref, back_ref, q_s, k_s, v_s, g_s, dk_s, dv_s):
    blocks = x_ref.shape[0] // message
    back = back_ref.shape[0] // blocks
    groups = blocks // LANES
    tile = SLOTS * LANES
    scale = LANES ** (-0.5)
    arrays = (q_s, k_s, v_s, g_s)
    rows_ref[...] = x_ref[...].astype(jnp.float32)
    key_at = SLOTS * (iota(tile, tile, 0) % LANES) + iota(tile, tile, 0) // LANES
    query_at = SLOTS * (iota(tile, tile, 1) % LANES) + iota(tile, tile, 1) // LANES
    causal = key_at <= query_at
    for head in range(per_dest):
        key_labels, query_labels = [], []
        for group in range(groups):
            first_row = group * LANES * message
            for array, scratch in enumerate(arrays):
                for slot in range(SLOTS):
                    row = first_row + (head * len(arrays) + array) * SLOTS + slot
                    at = (group * SLOTS + slot) * LANES
                    scratch[at : at + LANES, :] = rows_ref[
                        pl.ds(row, LANES, stride=message), :
                    ].astype(jnp.bfloat16)
            row = first_row + per_dest * len(arrays) * SLOTS + head
            label = rows_ref[pl.ds(row, LANES, stride=message), :]
            turned = jnp.transpose(label)
            half = LANES // 2
            key_labels.append(jnp.concatenate([label[:, :1], label[:, half : half + 1]], axis=0))
            row_label = jnp.concatenate([turned[:1, :], turned[half : half + 1, :]], axis=1)
            query_labels.append(jnp.where(row_label > 0.5, row_label, -1.0))
        dk_s[...] = jnp.zeros_like(dk_s)
        dv_s[...] = jnp.zeros_like(dv_s)
        for query_group in range(groups):
            own = slice(query_group * tile, (query_group + 1) * tile)
            q_rows, g_rows = q_s[own, :], g_s[own, :]
            scores = []
            row_max = jnp.full((1, tile), LOWEST_MAX, jnp.float32)
            for key_group in range(query_group + 1):
                keys = slice(key_group * tile, (key_group + 1) * tile)
                allowed = key_labels[key_group] == query_labels[query_group]
                if key_group == query_group:
                    allowed = allowed & causal
                score = jnp.where(allowed, dot_last(k_s[keys, :], q_rows) * scale, MASKED_SCORE)
                row_max = jnp.maximum(row_max, jnp.max(score, axis=0, keepdims=True))
                scores.append(score)
            total = jnp.zeros((1, tile), jnp.float32)
            weighted = jnp.zeros((1, tile), jnp.float32)
            raw, grads = [], []
            for key_group in range(query_group + 1):
                keys = slice(key_group * tile, (key_group + 1) * tile)
                weight = jnp.exp(scores[key_group] - row_max)
                prob_grad = dot_last(v_s[keys, :], g_rows)
                total = total + jnp.sum(weight, axis=0, keepdims=True)
                weighted = weighted + jnp.sum(weight * prob_grad, axis=0, keepdims=True)
                raw.append(weight)
                grads.append(prob_grad)
            inverse = 1.0 / jnp.maximum(total, 1.0)
            delta = weighted * inverse
            query_grad = jnp.zeros((LANES, tile), jnp.float32)
            for key_group in range(query_group + 1):
                keys = slice(key_group * tile, (key_group + 1) * tile)
                prob = raw[key_group] * inverse
                score_grad = (prob * (grads[key_group] - delta) * scale).astype(jnp.bfloat16)
                dv_s[keys, :] += dot(prob.astype(jnp.bfloat16), g_rows)
                dk_s[keys, :] += dot(score_grad, q_rows)
                query_grad = query_grad + lax.dot_general(
                    k_s[keys, :],
                    score_grad,
                    (((0,), (0,)), ((), ())),
                    preferred_element_type=jnp.float32,
                )
            query_rows = jnp.transpose(query_grad)
            for slot in range(SLOTS):
                row = query_group * LANES * back + head * 3 * SLOTS + slot
                back_ref[pl.ds(row, LANES, stride=back), :] = query_rows[
                    slot * LANES : (slot + 1) * LANES, :
                ]
        for array, grad in ((1, dk_s), (2, dv_s)):
            for group in range(groups):
                for slot in range(SLOTS):
                    row = group * LANES * back + (head * 3 + array) * SLOTS + slot
                    at = (group * SLOTS + slot) * LANES
                    back_ref[pl.ds(row, LANES, stride=back), :] = grad[at : at + LANES, :]
    out_ref[...] = back_ref[...].astype(jnp.bfloat16)


def unplace_kernel(owners, spills, y_ref, ids_ref, dq_ref, dk_ref, dv_ref, rows_ref):
    tokens, heads = ids_ref.shape
    per_dest = heads // spills
    outs = (dq_ref, dk_ref, dv_ref)
    back = per_dest * len(outs) * SLOTS
    owner_iota = iota(tokens, owners, 1)
    earlier = (iota(tokens, tokens, 1) < iota(tokens, tokens, 0)).astype(jnp.bfloat16)
    rows_ref[...] = y_ref[...].astype(jnp.float32)
    for head in range(heads):
        dest, within = divmod(head, per_dest)
        hot = ids_ref[:, head : head + 1] % owners == owner_iota
        count = dot(earlier, hot.astype(jnp.bfloat16))
        first = hot & (count < 0.5)
        second = hot & (count > 0.5)
        select = jnp.concatenate([first.astype(jnp.bfloat16), second.astype(jnp.bfloat16)], axis=1)
        stacked = []
        for array in range(len(outs)):
            slots = []
            for slot in range(SLOTS):
                row = dest * back + (within * len(outs) + array) * SLOTS + slot
                slots.append(rows_ref[pl.ds(row, owners, stride=spills * back), :])
            stacked.append(jnp.concatenate(slots, axis=0).astype(jnp.bfloat16))
        result = dot(select, jnp.concatenate(stacked, axis=1)).astype(jnp.bfloat16)
        for array, ref in enumerate(outs):
            ref[:, head * LANES : (head + 1) * LANES] = result[:, array * LANES : (array + 1) * LANES]


def local(queries, keys, values, out_grad, cluster_ids):
    tokens, width = queries.shape
    heads = cluster_ids.shape[1]
    owners = lax.axis_size("seq")
    spills = lax.axis_size("spill")
    devices = owners * spills
    per_dest = heads // spills
    message = per_dest * (4 * SLOTS + 1)
    back = per_dest * 3 * SLOTS
    whole = pl.BlockSpec(memory_space=pltpu.VMEM)
    params = pltpu.CompilerParams(vmem_limit_bytes=48 * 1024 * 1024)

    def exchange(rows, count):
        cut = rows.reshape(devices, count // SLOTS, SLOTS, LANES)
        moved = lax.all_to_all(cut, AXES, split_axis=0, concat_axis=0, tiled=True)
        return moved.reshape(devices * count, LANES)

    placed = pl.pallas_call(
        functools.partial(place_kernel, owners, spills),
        out_shape=jax.ShapeDtypeStruct((devices * message, LANES), jnp.bfloat16),
        in_specs=[whole] * 5,
        out_specs=whole,
        scratch_shapes=[pltpu.VMEM((devices * message, LANES), jnp.float32)],
        compiler_params=params,
        name="place",
    )(queries, keys, values, out_grad, cluster_ids)
    routed = exchange(placed, message)
    slots = devices * SLOTS
    returned = pl.pallas_call(
        functools.partial(attend_kernel, per_dest, message),
        out_shape=jax.ShapeDtypeStruct((devices * back, LANES), jnp.bfloat16),
        in_specs=[whole],
        out_specs=whole,
        scratch_shapes=[
            pltpu.VMEM((devices * message, LANES), jnp.float32),
            pltpu.VMEM((devices * back, LANES), jnp.float32),
        ]
        + [pltpu.VMEM((slots, LANES), jnp.bfloat16)] * 4
        + [pltpu.VMEM((slots, LANES), jnp.float32)] * 2,
        compiler_params=params,
        name="attend",
    )(routed)
    gradients = exchange(returned, back)
    grad_shape = jax.ShapeDtypeStruct((tokens, width), jnp.bfloat16)
    return pl.pallas_call(
        functools.partial(unplace_kernel, owners, spills),
        out_shape=(grad_shape, grad_shape, grad_shape),
        in_specs=[whole] * 2,
        out_specs=(whole, whole, whole),
        scratch_shapes=[pltpu.VMEM((devices * back, LANES), jnp.float32)],
        compiler_params=params,
        name="unplace",
    )(gradients, cluster_ids)


def solution(mesh):
    rows = P(AXES, None)
    return jax.shard_map(
        local,
        mesh=mesh,
        in_specs=(rows, rows, rows, rows, rows),
        out_specs=(rows, rows, rows),
        check_vma=False,
    )
```

```python
import functools
import math

import jax
import jax.numpy as jnp
from jax import lax
from jax.experimental import pallas as pl
from jax.experimental.pallas import tpu as pltpu
from jax.sharding import PartitionSpec as P

AXES = ("seq", "spill")
LANES = 128
SLOTS = 2
MASKED_SCORE = -1e30
LOWEST_MAX = -5e29
LOG2_E = math.log2(math.e)


def dot(left, right):
    return jnp.dot(left, right, preferred_element_type=jnp.float32)


def dot_last(left, right):
    return lax.dot_general(
        left, right, (((1,), (1,)), ((), ())), preferred_element_type=jnp.float32
    )


def iota(rows, columns, axis):
    return lax.broadcasted_iota(jnp.int32, (rows, columns), axis)


def choose(ids, owners, earlier):
    ids = jnp.broadcast_to(ids, (owners, ids.shape[1]))
    hot = ids % owners == iota(owners, ids.shape[1], 0)
    count = dot(hot.astype(jnp.bfloat16), earlier)
    return hot & (count < 0.5), hot & (count > 0.5), (ids // owners + 1).astype(jnp.float32)


def place_kernel(
    owners, spills, q_hbm, k_hbm, v_hbm, g_hbm, ids_hbm, out_ref, q_ref, k_ref, v_ref, g_ref, ids_ref, rows_ref, sems
):
    heads, tokens = ids_ref.shape
    ids_copy = pltpu.make_async_copy(ids_hbm, ids_ref, sems.at[4 * spills])
    ids_copy.start()
    per_dest = heads // spills
    width = per_dest * LANES
    arrays = (q_ref, k_ref, v_ref, g_ref)
    copies = []
    for dest in range(spills):
        columns = slice(dest * width, (dest + 1) * width)
        for array, (source, target) in enumerate(zip((q_hbm, k_hbm, v_hbm, g_hbm), arrays)):
            copies.append(
                pltpu.make_async_copy(
                    source.at[:, columns], target.at[:, columns], sems.at[dest * len(arrays) + array]
                )
            )
            copies[-1].start()
    data_rows = per_dest * len(arrays) * SLOTS
    message = data_rows + per_dest
    earlier = (iota(tokens, tokens, 0) < iota(tokens, tokens, 1)).astype(jnp.bfloat16)
    first_lanes = iota(owners, LANES, 1) < LANES // 2
    ids_copy.wait()
    for head in range(heads):
        dest, within = divmod(head, per_dest)
        first, second, label = choose(ids_ref[head : head + 1, :], owners, earlier)
        select = jnp.concatenate([first.astype(jnp.bfloat16), second.astype(jnp.bfloat16)], axis=0)
        base = dest * message
        first_label = jnp.sum(jnp.where(first, label, 0.0), axis=1, keepdims=True)
        second_label = jnp.sum(jnp.where(second, label, 0.0), axis=1, keepdims=True)
        rows_ref[pl.ds(base + data_rows + within, owners, stride=spills * message), :] = jnp.where(
            first_lanes, first_label, second_label
        )
        if within == 0:
            for copy in copies[dest * len(arrays) : (dest + 1) * len(arrays)]:
                copy.wait()
        columns = slice(head * LANES, (head + 1) * LANES)
        placed = dot(select, jnp.concatenate([ref[:, columns] for ref in arrays], axis=1))
        for array in range(len(arrays)):
            for slot in range(SLOTS):
                row = base + (within * len(arrays) + array) * SLOTS + slot
                rows_ref[pl.ds(row, owners, stride=spills * message), :] = placed[
                    slot * owners : (slot + 1) * owners, array * LANES : (array + 1) * LANES
                ]
    out_ref[...] = rows_ref[...].astype(jnp.bfloat16)


def attend_kernel(per_dest, message, x_ref, out_ref, rows_ref, back_ref, q_s, k_s, v_s, g_s, dk_s, dv_s):
    blocks = x_ref.shape[0] // message
    back = back_ref.shape[0] // blocks
    groups = blocks // LANES
    tile = SLOTS * LANES
    scale = LANES ** (-0.5)
    arrays = (q_s, k_s, v_s, g_s)
    rows_ref[...] = x_ref[...].astype(jnp.float32)
    key_at = SLOTS * (iota(tile, tile, 0) % LANES) + iota(tile, tile, 0) // LANES
    query_at = SLOTS * (iota(tile, tile, 1) % LANES) + iota(tile, tile, 1) // LANES
    causal = key_at <= query_at
    for head in range(per_dest):
        key_labels, query_labels = [], []
        for group in range(groups):
            first_row = group * LANES * message
            for array, scratch in enumerate(arrays):
                for slot in range(SLOTS):
                    row = first_row + (head * len(arrays) + array) * SLOTS + slot
                    at = (group * SLOTS + slot) * LANES
                    scratch[at : at + LANES, :] = rows_ref[
                        pl.ds(row, LANES, stride=message), :
                    ].astype(jnp.bfloat16)
            row = first_row + per_dest * len(arrays) * SLOTS + head
            label = rows_ref[pl.ds(row, LANES, stride=message), :]
            turned = jnp.transpose(label)
            half = LANES // 2
            key_labels.append(jnp.concatenate([label[:, :1], label[:, half : half + 1]], axis=0))
            row_label = jnp.concatenate([turned[:1, :], turned[half : half + 1, :]], axis=1)
            query_labels.append(jnp.where(row_label > 0.5, row_label, -1.0))
        dk_s[...] = jnp.zeros_like(dk_s)
        dv_s[...] = jnp.zeros_like(dv_s)
        for query_group in range(groups):
            own = slice(query_group * tile, (query_group + 1) * tile)
            q_rows, g_rows = q_s[own, :], g_s[own, :]
            scores = []
            row_max = jnp.full((1, tile), LOWEST_MAX, jnp.float32)
            for key_group in range(query_group + 1):
                keys = slice(key_group * tile, (key_group + 1) * tile)
                allowed = key_labels[key_group] == query_labels[query_group]
                if key_group == query_group:
                    allowed = allowed & causal
                score = jnp.where(allowed, dot_last(k_s[keys, :], q_rows), MASKED_SCORE)
                row_max = jnp.maximum(row_max, jnp.max(score, axis=0, keepdims=True))
                scores.append(score)
            total = jnp.zeros((1, tile), jnp.float32)
            weighted = jnp.zeros((1, tile), jnp.float32)
            raw, grads = [], []
            for key_group in range(query_group + 1):
                keys = slice(key_group * tile, (key_group + 1) * tile)
                weight = jnp.exp2((scores[key_group] - row_max) * (scale * LOG2_E))
                prob_grad = dot_last(v_s[keys, :], g_rows)
                total = total + jnp.sum(weight, axis=0, keepdims=True)
                weighted = weighted + jnp.sum(weight * prob_grad, axis=0, keepdims=True)
                raw.append(weight)
                grads.append(prob_grad)
            inverse = 1.0 / jnp.maximum(total, 1.0)
            delta = weighted * inverse
            query_grad = jnp.zeros((LANES, tile), jnp.float32)
            for key_group in range(query_group + 1):
                keys = slice(key_group * tile, (key_group + 1) * tile)
                prob = raw[key_group] * inverse
                score_grad = (prob * (grads[key_group] - delta)).astype(jnp.bfloat16)
                dv_s[keys, :] += dot(prob.astype(jnp.bfloat16), g_rows)
                dk_s[keys, :] += dot(score_grad, q_rows)
                query_grad = query_grad + lax.dot_general(
                    k_s[keys, :],
                    score_grad,
                    (((0,), (0,)), ((), ())),
                    preferred_element_type=jnp.float32,
                )
            query_rows = jnp.transpose(query_grad) * scale
            for slot in range(SLOTS):
                row = query_group * LANES * back + head * 3 * SLOTS + slot
                back_ref[pl.ds(row, LANES, stride=back), :] = query_rows[
                    slot * LANES : (slot + 1) * LANES, :
                ]
        for array, grad, factor in ((1, dk_s, scale), (2, dv_s, 1.0)):
            for group in range(groups):
                for slot in range(SLOTS):
                    row = group * LANES * back + (head * 3 + array) * SLOTS + slot
                    at = (group * SLOTS + slot) * LANES
                    back_ref[pl.ds(row, LANES, stride=back), :] = grad[at : at + LANES, :] * factor
    out_ref[...] = back_ref[...].astype(jnp.bfloat16)


def unplace_kernel(owners, spills, y_ref, ids_ref, dq_hbm, dk_hbm, dv_hbm, rows_ref, dq_ref, dk_ref, dv_ref, sems):
    heads, tokens = ids_ref.shape
    per_dest = heads // spills
    width = per_dest * LANES
    outs = (dq_ref, dk_ref, dv_ref)
    back = per_dest * len(outs) * SLOTS
    owner_iota = iota(tokens, owners, 1)
    earlier = (iota(tokens, tokens, 1) < iota(tokens, tokens, 0)).astype(jnp.bfloat16)
    ids = jnp.transpose(ids_ref[...].astype(jnp.float32)).astype(jnp.int32)
    rows_ref[...] = y_ref[...].astype(jnp.float32)
    copies = []
    for head in range(heads):
        dest, within = divmod(head, per_dest)
        hot = ids[:, head : head + 1] % owners == owner_iota
        count = dot(earlier, hot.astype(jnp.bfloat16))
        first = hot & (count < 0.5)
        second = hot & (count > 0.5)
        select = jnp.concatenate([first.astype(jnp.bfloat16), second.astype(jnp.bfloat16)], axis=1)
        stacked = []
        for array in range(len(outs)):
            slots = []
            for slot in range(SLOTS):
                row = dest * back + (within * len(outs) + array) * SLOTS + slot
                slots.append(rows_ref[pl.ds(row, owners, stride=spills * back), :])
            stacked.append(jnp.concatenate(slots, axis=0).astype(jnp.bfloat16))
        result = dot(select, jnp.concatenate(stacked, axis=1)).astype(jnp.bfloat16)
        for array, ref in enumerate(outs):
            ref[:, head * LANES : (head + 1) * LANES] = result[:, array * LANES : (array + 1) * LANES]
        if within == per_dest - 1:
            columns = slice(dest * width, (dest + 1) * width)
            for array, (source, target) in enumerate(zip(outs, (dq_hbm, dk_hbm, dv_hbm))):
                copies.append(
                    pltpu.make_async_copy(
                        source.at[:, columns], target.at[:, columns], sems.at[dest * len(outs) + array]
                    )
                )
                copies[-1].start()
    for copy in copies:
        copy.wait()


def local_ops(owners, spills, tokens, heads):
    devices = owners * spills
    per_dest = heads // spills
    message = per_dest * (4 * SLOTS + 1)
    back = per_dest * 3 * SLOTS
    slots = devices * SLOTS
    width = heads * LANES
    whole = pl.BlockSpec(memory_space=pltpu.VMEM)
    hbm = pl.BlockSpec(memory_space=pltpu.HBM)
    params = pltpu.CompilerParams(vmem_limit_bytes=48 * 1024 * 1024)
    token_rows = pltpu.VMEM((tokens, width), jnp.bfloat16)
    grad_shape = jax.ShapeDtypeStruct((tokens, width), jnp.bfloat16)
    place = pl.pallas_call(
        functools.partial(place_kernel, owners, spills),
        out_shape=jax.ShapeDtypeStruct((devices * message, LANES), jnp.bfloat16),
        in_specs=[hbm] * 5,
        out_specs=whole,
        scratch_shapes=[token_rows] * 4
        + [
            pltpu.VMEM((heads, tokens), jnp.int32),
            pltpu.VMEM((devices * message, LANES), jnp.float32),
            pltpu.SemaphoreType.DMA((4 * spills + 1,)),
        ],
        compiler_params=params,
        name="place",
    )
    attend = pl.pallas_call(
        functools.partial(attend_kernel, per_dest, message),
        out_shape=jax.ShapeDtypeStruct((devices * back, LANES), jnp.bfloat16),
        in_specs=[whole],
        out_specs=whole,
        scratch_shapes=[
            pltpu.VMEM((devices * message, LANES), jnp.float32),
            pltpu.VMEM((devices * back, LANES), jnp.float32),
        ]
        + [pltpu.VMEM((slots, LANES), jnp.bfloat16)] * 4
        + [pltpu.VMEM((slots, LANES), jnp.float32)] * 2,
        compiler_params=params,
        name="attend",
    )
    unplace = pl.pallas_call(
        functools.partial(unplace_kernel, owners, spills),
        out_shape=(grad_shape, grad_shape, grad_shape),
        in_specs=[whole] * 2,
        out_specs=(hbm, hbm, hbm),
        scratch_shapes=[pltpu.VMEM((devices * back, LANES), jnp.float32)]
        + [token_rows] * 3
        + [pltpu.SemaphoreType.DMA((3 * spills,))],
        compiler_params=params,
        name="unplace",
    )
    return place, attend, unplace


def local(queries, keys, values, out_grad, cluster_ids):
    owners, spills = lax.axis_size("seq"), lax.axis_size("spill")
    devices = owners * spills
    place, attend, unplace = local_ops(owners, spills, *cluster_ids.shape)

    def exchange(rows):
        cut = rows.reshape(devices, -1, SLOTS, LANES)
        moved = lax.all_to_all(cut, AXES, split_axis=0, concat_axis=0, tiled=True)
        return moved.reshape(rows.shape)

    ids = jnp.transpose(cluster_ids)
    inputs = (queries, keys, values, out_grad, ids)
    routed = exchange(place(*(pltpu.with_memory_space_constraint(x, pltpu.HBM) for x in inputs)))
    return unplace(exchange(attend(routed)), ids)


def solution(mesh):
    rows = P(AXES, None)
    return jax.shard_map(
        local,
        mesh=mesh,
        in_specs=(rows, rows, rows, rows, rows),
        out_specs=(rows, rows, rows),
        check_vma=False,
    )
```

```python
import functools
import math

import jax
import jax.numpy as jnp
from jax import lax
from jax.experimental import pallas as pl
from jax.experimental.pallas import tpu as pltpu
from jax.sharding import PartitionSpec as P

AXES = ("seq", "spill")
LANES = 128
SLOTS = 2
FOLD = 8
MASKED_SCORE = -1e30
LOWEST_MAX = -5e29
LOG2_E = math.log2(math.e)


def dot(left, right):
    return jnp.dot(left, right, preferred_element_type=jnp.float32)


def dot_last(left, right):
    return lax.dot_general(
        left, right, (((1,), (1,)), ((), ())), preferred_element_type=jnp.float32
    )


def iota(rows, columns, axis):
    return lax.broadcasted_iota(jnp.int32, (rows, columns), axis)


def one_hot_pair(hot, count, axis):
    first = jnp.where(hot & (count < 0.5), 1.0, 0.0)
    second = jnp.where(hot & (count > 0.5), 1.0, 0.0)
    return first, second, jnp.concatenate([first, second], axis=axis).astype(jnp.bfloat16)


def place_kernel(
    owners,
    spills,
    q_hbm,
    k_hbm,
    v_hbm,
    g_hbm,
    ids_hbm,
    out_ref,
    return_ref,
    q_ref,
    k_ref,
    v_ref,
    g_ref,
    ids_ref,
    select_ref,
    rows_ref,
    sems,
):
    heads, tokens = ids_ref.shape
    per_dest = heads // spills
    width = per_dest * LANES
    arrays = (q_ref, k_ref, v_ref, g_ref)
    ids_copy = pltpu.make_async_copy(ids_hbm, ids_ref, sems.at[len(arrays) * spills])
    ids_copy.start()
    copies = []
    for dest in range(spills):
        columns = slice(dest * width, (dest + 1) * width)
        for array, (source, target) in enumerate(zip((q_hbm, k_hbm, v_hbm, g_hbm), arrays)):
            copies.append(
                pltpu.make_async_copy(
                    source.at[:, columns], target.at[:, columns], sems.at[dest * len(arrays) + array]
                )
            )
            copies[-1].start()
    data_rows = per_dest * len(arrays) * SLOTS
    message = data_rows + SLOTS
    token_before = iota(tokens, tokens, 0) < iota(tokens, tokens, 1)
    before = jnp.where(token_before, 1.0, 0.0).astype(jnp.bfloat16)
    after = jnp.where(iota(tokens, tokens, 1) < iota(tokens, tokens, 0), 1.0, 0.0).astype(jnp.bfloat16)
    half_lanes = iota(owners, LANES, 1) // (LANES // per_dest)
    ids_copy.wait()
    id_columns = jnp.transpose(ids_ref[...].astype(jnp.float32)).astype(jnp.int32)
    for dest in range(spills):
        slot_labels = [jnp.zeros((owners, LANES), jnp.float32)] * SLOTS
        for within in range(per_dest):
            head = dest * per_dest + within
            ids = jnp.broadcast_to(ids_ref[head : head + 1, :], (owners, tokens))
            hot = ids % owners == iota(owners, tokens, 0)
            count = dot(jnp.where(hot, 1.0, 0.0).astype(jnp.bfloat16), before)
            first, second, select = one_hot_pair(hot, count, 0)
            select_ref[head * SLOTS * owners : (head + 1) * SLOTS * owners, :] = select
            label = (ids // owners + 1).astype(jnp.float32)
            for slot, mask in enumerate((first, second)):
                slot_label = jnp.sum(mask * label, axis=1, keepdims=True)
                slot_labels[slot] = jnp.where(half_lanes == within, slot_label, slot_labels[slot])
            hot = id_columns[:, head : head + 1] % owners == iota(tokens, owners, 1)
            count = dot(after, jnp.where(hot, 1.0, 0.0).astype(jnp.bfloat16))
            return_ref[head * tokens : (head + 1) * tokens, :] = one_hot_pair(hot, count, 1)[2]
        for slot in range(SLOTS):
            row = dest * message + data_rows + slot
            rows_ref[pl.ds(row, owners, stride=spills * message), :] = slot_labels[slot]
    for head in range(heads):
        dest, within = divmod(head, per_dest)
        if within == 0:
            for copy in copies[dest * len(arrays) : (dest + 1) * len(arrays)]:
                copy.wait()
        columns = slice(head * LANES, (head + 1) * LANES)
        placed = dot(
            select_ref[head * SLOTS * owners : (head + 1) * SLOTS * owners, :],
            jnp.concatenate([ref[:, columns] for ref in arrays], axis=1),
        )
        for array in range(len(arrays)):
            for slot in range(SLOTS):
                row = dest * message + (within * len(arrays) + array) * SLOTS + slot
                rows_ref[pl.ds(row, owners, stride=spills * message), :] = placed[
                    slot * owners : (slot + 1) * owners, array * LANES : (array + 1) * LANES
                ]
    out_ref[...] = rows_ref[...].astype(jnp.bfloat16)


def attend_kernel(
    per_dest, message, x_ref, out_ref, rows_ref, back_ref, q_s, k_s, v_s, g_s, labels_s, dk_s, dv_s
):
    blocks = x_ref.shape[0] // message
    back = back_ref.shape[0] // blocks
    groups = blocks // LANES
    tile = SLOTS * LANES
    slots = blocks * SLOTS
    scale = LANES ** (-0.5)
    arrays = (q_s, k_s, v_s, g_s)
    rows_ref[...] = x_ref[...].astype(jnp.float32)
    key_at = SLOTS * (iota(tile, tile, 0) % LANES) + iota(tile, tile, 0) // LANES
    query_at = SLOTS * (iota(tile, tile, 1) % LANES) + iota(tile, tile, 1) // LANES
    causal = key_at <= query_at
    query_labels = [[None] * groups for _ in range(per_dest)]
    for group in range(groups):
        first_row = group * LANES * message
        for slot in range(SLOTS):
            at = (group * SLOTS + slot) * LANES
            for head in range(per_dest):
                for array, scratch in enumerate(arrays):
                    row = first_row + (head * len(arrays) + array) * SLOTS + slot
                    scratch[head * slots + at : head * slots + at + LANES, :] = rows_ref[
                        pl.ds(row, LANES, stride=message), :
                    ].astype(jnp.bfloat16)
            row = first_row + per_dest * len(arrays) * SLOTS + slot
            label = rows_ref[pl.ds(row, LANES, stride=message), :]
            turned = jnp.transpose(label)
            for head in range(per_dest):
                lane = head * (LANES // per_dest)
                labels_s[head * slots + at : head * slots + at + LANES, :] = jnp.broadcast_to(
                    label[:, lane : lane + 1], (LANES, LANES)
                )
                part = turned[lane : lane + 1, :]
                part = jnp.where(part > 0.5, part, -1.0)
                before = query_labels[head][group]
                query_labels[head][group] = part if slot == 0 else jnp.concatenate([before, part], axis=1)

    def tile_of(head, group):
        start = head * slots + group * tile
        return slice(start, start + tile)

    def score_stage(head, query_group):
        q_rows = q_s[tile_of(head, query_group), :]
        query_label = query_labels[head][query_group]
        scores = []
        highest = jnp.full((FOLD, tile), LOWEST_MAX, jnp.float32)
        for key_group in range(query_group + 1):
            raw = dot_last(k_s[tile_of(head, key_group), :], q_rows)
            start = head * slots + key_group * tile
            kept = []
            for at in range(0, tile, FOLD):
                key_label = labels_s[start + at : start + at + FOLD, :]
                allowed = jnp.concatenate([key_label, key_label], axis=1) == query_label
                if key_group == query_group:
                    allowed = allowed & causal[at : at + FOLD, :]
                kept.append(jnp.where(allowed, raw[at : at + FOLD, :], MASKED_SCORE))
                highest = jnp.maximum(highest, kept[-1])
            scores.append(kept)
        return scores, jnp.max(highest, axis=0, keepdims=True)

    def gradient_stage(head, query_group, scores, row_max):
        own = tile_of(head, query_group)
        q_rows, g_rows = q_s[own, :], g_s[own, :]
        total = jnp.zeros((FOLD, tile), jnp.float32)
        weighted = jnp.zeros((FOLD, tile), jnp.float32)
        weights, grads = [], []
        for key_group in range(query_group + 1):
            prob_grad = dot_last(v_s[tile_of(head, key_group), :], g_rows)
            kept, split = [], []
            for index, at in enumerate(range(0, tile, FOLD)):
                weight = jnp.exp2((scores[key_group][index] - row_max) * (scale * LOG2_E))
                grad = prob_grad[at : at + FOLD, :]
                total = total + weight
                weighted = weighted + weight * grad
                kept.append(weight)
                split.append(grad)
            weights.append(kept)
            grads.append(split)
        inverse = 1.0 / jnp.maximum(jnp.sum(total, axis=0, keepdims=True), 1.0)
        delta = jnp.sum(weighted, axis=0, keepdims=True) * inverse
        query_grad = jnp.zeros((LANES, tile), jnp.float32)
        for key_group in range(query_group + 1):
            keys = tile_of(head, key_group)
            probs, score_grads = [], []
            for index in range(0, tile // FOLD, 2):
                pair = []
                for part in (index, index + 1):
                    prob = weights[key_group][part] * inverse
                    pair.append((prob, prob * (grads[key_group][part] - delta)))
                probs.append(jnp.concatenate([pair[0][0], pair[1][0]], axis=0).astype(jnp.bfloat16))
                score_grads.append(jnp.concatenate([pair[0][1], pair[1][1]], axis=0).astype(jnp.bfloat16))
            prob = jnp.concatenate(probs, axis=0)
            score_grad = jnp.concatenate(score_grads, axis=0)
            value_part = dot(prob, g_rows)
            key_part = dot(score_grad, q_rows)
            if key_group == query_group:
                dv_s[keys, :] = value_part
                dk_s[keys, :] = key_part
            else:
                dv_s[keys, :] += value_part
                dk_s[keys, :] += key_part
            query_grad = query_grad + lax.dot_general(
                k_s[keys, :],
                score_grad,
                (((0,), (0,)), ((), ())),
                preferred_element_type=jnp.float32,
            )
        query_rows = jnp.transpose(query_grad) * scale
        for slot in range(SLOTS):
            row = query_group * LANES * back + head * 3 * SLOTS + slot
            back_ref[pl.ds(row, LANES, stride=back), :] = query_rows[slot * LANES : (slot + 1) * LANES, :]

    units = [(head, group) for group in range(groups) for head in range(per_dest)]
    ahead = score_stage(*units[0])
    for index, unit in enumerate(units):
        scores, row_max = ahead
        if index + 1 < len(units):
            ahead = score_stage(*units[index + 1])
        gradient_stage(*unit, scores, row_max)
    for head in range(per_dest):
        for array, grad, factor in ((1, dk_s, scale), (2, dv_s, 1.0)):
            for group in range(groups):
                for slot in range(SLOTS):
                    row = group * LANES * back + (head * 3 + array) * SLOTS + slot
                    at = head * slots + (group * SLOTS + slot) * LANES
                    back_ref[pl.ds(row, LANES, stride=back), :] = grad[at : at + LANES, :] * factor
    out_ref[...] = back_ref[...].astype(jnp.bfloat16)


def unplace_kernel(
    owners, spills, y_ref, select_ref, dq_hbm, dk_hbm, dv_hbm, rows_ref, dq_ref, dk_ref, dv_ref, sems
):
    tokens = dq_ref.shape[0]
    heads = select_ref.shape[0] // tokens
    per_dest = heads // spills
    width = per_dest * LANES
    outs = (dq_ref, dk_ref, dv_ref)
    back = per_dest * len(outs) * SLOTS
    rows_ref[...] = y_ref[...].astype(jnp.float32)
    copies = []
    for head in range(heads):
        dest, within = divmod(head, per_dest)
        stacked = []
        for array in range(len(outs)):
            slots = []
            for slot in range(SLOTS):
                row = dest * back + (within * len(outs) + array) * SLOTS + slot
                slots.append(rows_ref[pl.ds(row, owners, stride=spills * back), :])
            stacked.append(jnp.concatenate(slots, axis=0).astype(jnp.bfloat16))
        select = select_ref[head * tokens : (head + 1) * tokens, :]
        result = dot(select, jnp.concatenate(stacked, axis=1)).astype(jnp.bfloat16)
        for array, ref in enumerate(outs):
            ref[:, head * LANES : (head + 1) * LANES] = result[:, array * LANES : (array + 1) * LANES]
        if within == per_dest - 1:
            columns = slice(dest * width, (dest + 1) * width)
            for array, (source, target) in enumerate(zip(outs, (dq_hbm, dk_hbm, dv_hbm))):
                copies.append(
                    pltpu.make_async_copy(
                        source.at[:, columns], target.at[:, columns], sems.at[dest * len(outs) + array]
                    )
                )
                copies[-1].start()
    for copy in copies:
        copy.wait()


def local_ops(owners, spills, tokens, heads):
    devices = owners * spills
    per_dest = heads // spills
    message = per_dest * 4 * SLOTS + SLOTS
    back = per_dest * 3 * SLOTS
    slots = devices * SLOTS
    width = heads * LANES
    whole = pl.BlockSpec(memory_space=pltpu.VMEM)
    hbm = pl.BlockSpec(memory_space=pltpu.HBM)
    params = pltpu.CompilerParams(vmem_limit_bytes=48 * 1024 * 1024)
    token_rows = pltpu.VMEM((tokens, width), jnp.bfloat16)
    grad_shape = jax.ShapeDtypeStruct((tokens, width), jnp.bfloat16)
    place = pl.pallas_call(
        functools.partial(place_kernel, owners, spills),
        out_shape=(
            jax.ShapeDtypeStruct((devices * message, LANES), jnp.bfloat16),
            jax.ShapeDtypeStruct((heads * tokens, SLOTS * owners), jnp.bfloat16),
        ),
        in_specs=[hbm] * 5,
        out_specs=(whole, whole),
        scratch_shapes=[token_rows] * 4
        + [
            pltpu.VMEM((heads, tokens), jnp.int32),
            pltpu.VMEM((heads * SLOTS * owners, tokens), jnp.bfloat16),
            pltpu.VMEM((devices * message, LANES), jnp.float32),
            pltpu.SemaphoreType.DMA((4 * spills + 1,)),
        ],
        compiler_params=params,
        name="place",
    )
    attend = pl.pallas_call(
        functools.partial(attend_kernel, per_dest, message),
        out_shape=jax.ShapeDtypeStruct((devices * back, LANES), jnp.bfloat16),
        in_specs=[whole],
        out_specs=whole,
        scratch_shapes=[
            pltpu.VMEM((devices * message, LANES), jnp.float32),
            pltpu.VMEM((devices * back, LANES), jnp.float32),
            pltpu.VMEM((per_dest * slots, LANES), jnp.bfloat16),
            pltpu.VMEM((per_dest * slots, LANES), jnp.bfloat16),
            pltpu.VMEM((per_dest * slots, LANES), jnp.bfloat16),
            pltpu.VMEM((per_dest * slots, LANES), jnp.bfloat16),
            pltpu.VMEM((per_dest * slots, LANES), jnp.float32),
            pltpu.VMEM((per_dest * slots, LANES), jnp.float32),
            pltpu.VMEM((per_dest * slots, LANES), jnp.float32),
        ],
        compiler_params=params,
        name="attend",
    )
    unplace = pl.pallas_call(
        functools.partial(unplace_kernel, owners, spills),
        out_shape=(grad_shape, grad_shape, grad_shape),
        in_specs=[whole] * 2,
        out_specs=(hbm, hbm, hbm),
        scratch_shapes=[pltpu.VMEM((devices * back, LANES), jnp.float32)]
        + [token_rows] * 3
        + [pltpu.SemaphoreType.DMA((3 * spills,))],
        compiler_params=params,
        name="unplace",
    )
    return place, attend, unplace


def local(queries, keys, values, out_grad, cluster_ids):
    owners, spills = lax.axis_size("seq"), lax.axis_size("spill")
    devices = owners * spills
    place, attend, unplace = local_ops(owners, spills, *cluster_ids.shape)

    def exchange(rows):
        cut = rows.reshape(devices, -1, SLOTS, LANES)
        moved = lax.all_to_all(cut, AXES, split_axis=0, concat_axis=0, tiled=True)
        return moved.reshape(rows.shape)

    inputs = (queries, keys, values, out_grad, jnp.transpose(cluster_ids))
    rows, select = place(*(pltpu.with_memory_space_constraint(x, pltpu.HBM) for x in inputs))
    return unplace(exchange(attend(exchange(rows))), select)


def solution(mesh):
    rows = P(AXES, None)
    return jax.shard_map(
        local,
        mesh=mesh,
        in_specs=(rows, rows, rows, rows, rows),
        out_specs=(rows, rows, rows),
        check_vma=False,
    )
```

```python
import functools
import math

import jax
import jax.numpy as jnp
from jax import lax
from jax.experimental import pallas as pl
from jax.experimental.pallas import tpu as pltpu
from jax.sharding import PartitionSpec as P

RUN = 16
AXES = ("outer", "inner", "spill")
ROUTE = ("outer", "spill", "inner")
LANES = 128
SLOTS = 2
FOLD = 8
MASKED_SCORE = -1e30
LOWEST_MAX = -5e29
LOG2_E = math.log2(math.e)


def dot(left, right):
    return jnp.dot(left, right, preferred_element_type=jnp.float32)


def dot_last(left, right):
    return lax.dot_general(
        left, right, (((1,), (1,)), ((), ())), preferred_element_type=jnp.float32
    )


def iota(rows, columns, axis):
    return lax.broadcasted_iota(jnp.int32, (rows, columns), axis)


def one_hot_pair(hot, count, axis):
    first = jnp.where(hot & (count < 0.5), 1.0, 0.0)
    second = jnp.where(hot & (count > 0.5), 1.0, 0.0)
    return first, second, jnp.concatenate([first, second], axis=axis).astype(jnp.bfloat16)


def run_rows(spills, rows, run, spill, row):
    return pl.ds((run * spills + spill) * RUN * rows + row, RUN, stride=rows)


def place_kernel(
    owners,
    spills,
    q_hbm,
    k_hbm,
    v_hbm,
    g_hbm,
    ids_hbm,
    out_ref,
    return_ref,
    q_ref,
    k_ref,
    v_ref,
    g_ref,
    ids_ref,
    select_ref,
    rows_ref,
    sems,
):
    heads, tokens = ids_ref.shape
    per_dest = heads // spills
    width = per_dest * LANES
    arrays = (q_ref, k_ref, v_ref, g_ref)
    ids_copy = pltpu.make_async_copy(ids_hbm, ids_ref, sems.at[len(arrays) * spills])
    ids_copy.start()
    copies = []
    for dest in range(spills):
        columns = slice(dest * width, (dest + 1) * width)
        for array, (source, target) in enumerate(zip((q_hbm, k_hbm, v_hbm, g_hbm), arrays)):
            copies.append(
                pltpu.make_async_copy(
                    source.at[:, columns], target.at[:, columns], sems.at[dest * len(arrays) + array]
                )
            )
            copies[-1].start()
    data_rows = per_dest * len(arrays) * SLOTS
    message = data_rows + SLOTS
    token_before = iota(tokens, tokens, 0) < iota(tokens, tokens, 1)
    before = jnp.where(token_before, 1.0, 0.0).astype(jnp.bfloat16)
    after = jnp.where(iota(tokens, tokens, 1) < iota(tokens, tokens, 0), 1.0, 0.0).astype(jnp.bfloat16)
    half_lanes = iota(owners, LANES, 1) // (LANES // per_dest)
    ids_copy.wait()
    ids = ids_ref[...]
    all_owners = ids % owners
    all_labels = (ids // owners + 1).astype(jnp.float32)
    owner_columns = jnp.transpose(all_owners.astype(jnp.float32)).astype(jnp.int32)
    for dest in range(spills):
        slot_labels = [jnp.zeros((owners, LANES), jnp.float32)] * SLOTS
        for within in range(per_dest):
            head = dest * per_dest + within
            hot = all_owners[head : head + 1, :] == iota(owners, tokens, 0)
            count = dot(jnp.where(hot, 1.0, 0.0).astype(jnp.bfloat16), before)
            first, second, select = one_hot_pair(hot, count, 0)
            select_ref[head * SLOTS * owners : (head + 1) * SLOTS * owners, :] = select
            label = all_labels[head : head + 1, :]
            for slot, mask in enumerate((first, second)):
                slot_label = jnp.sum(mask * label, axis=1, keepdims=True)
                slot_labels[slot] = jnp.where(half_lanes == within, slot_label, slot_labels[slot])
            hot = owner_columns[:, head : head + 1] == iota(tokens, owners, 1)
            count = dot(after, jnp.where(hot, 1.0, 0.0).astype(jnp.bfloat16))
            return_ref[head * tokens : (head + 1) * tokens, :] = one_hot_pair(hot, count, 1)[2]
        for slot in range(SLOTS):
            for run in range(owners // RUN):
                rows_ref[run_rows(spills, message, run, dest, data_rows + slot), :] = slot_labels[slot][
                    run * RUN : (run + 1) * RUN, :
                ]
    for head in range(heads):
        dest, within = divmod(head, per_dest)
        if within == 0:
            for copy in copies[dest * len(arrays) : (dest + 1) * len(arrays)]:
                copy.wait()
        columns = slice(head * LANES, (head + 1) * LANES)
        placed = dot(
            select_ref[head * SLOTS * owners : (head + 1) * SLOTS * owners, :],
            jnp.concatenate([ref[:, columns] for ref in arrays], axis=1),
        )
        for array in range(len(arrays)):
            for slot in range(SLOTS):
                row = (within * len(arrays) + array) * SLOTS + slot
                for run in range(owners // RUN):
                    at = slot * owners + run * RUN
                    rows_ref[run_rows(spills, message, run, dest, row), :] = placed[
                        at : at + RUN, array * LANES : (array + 1) * LANES
                    ]
    out_ref[...] = rows_ref[...].astype(jnp.bfloat16)


def attend_kernel(
    spills, per_dest, message, x_ref, out_ref, rows_ref, back_ref, q_s, k_s, v_s, g_s, labels_s, dk_s, dv_s
):
    blocks = x_ref.shape[0] // message
    back = back_ref.shape[0] // blocks
    groups = blocks // LANES
    tile = SLOTS * LANES
    slots = blocks * SLOTS
    scale = LANES ** (-0.5)
    arrays = (q_s, k_s, v_s, g_s)
    rows_ref[...] = x_ref[...].astype(jnp.float32)

    def position(rows, columns, axis):
        index = iota(rows, columns, axis)
        block = index % LANES
        run, spill = block // (spills * RUN), block // RUN % spills
        return SLOTS * (spills * (run * RUN + block % RUN) + spill) + index // LANES

    key_position = position(tile, LANES, 0)
    query_position = position(FOLD, tile, 1)
    query_labels = [[None] * groups for _ in range(per_dest)]
    for group in range(groups):
        first_row = group * LANES * message
        for slot in range(SLOTS):
            at = (group * SLOTS + slot) * LANES
            for head in range(per_dest):
                for array, scratch in enumerate(arrays):
                    row = first_row + (head * len(arrays) + array) * SLOTS + slot
                    scratch[head * slots + at : head * slots + at + LANES, :] = rows_ref[
                        pl.ds(row, LANES, stride=message), :
                    ].astype(jnp.bfloat16)
            row = first_row + per_dest * len(arrays) * SLOTS + slot
            label = rows_ref[pl.ds(row, LANES, stride=message), :]
            turned = jnp.transpose(label)
            for head in range(per_dest):
                lane = head * (LANES // per_dest)
                labels_s[head * slots + at : head * slots + at + LANES, :] = jnp.broadcast_to(
                    label[:, lane : lane + 1], (LANES, LANES)
                )
                part = turned[lane : lane + 1, :]
                part = jnp.where(part > 0.5, part, -1.0)
                before = query_labels[head][group]
                query_labels[head][group] = part if slot == 0 else jnp.concatenate([before, part], axis=1)

    def tile_of(head, group):
        start = head * slots + group * tile
        return slice(start, start + tile)

    def score_stage(head, query_group):
        q_rows = q_s[tile_of(head, query_group), :]
        query_label = query_labels[head][query_group]
        scores = []
        highest = jnp.full((FOLD, tile), LOWEST_MAX, jnp.float32)
        for key_group in range(query_group + 1):
            raw = dot_last(k_s[tile_of(head, key_group), :], q_rows)
            start = head * slots + key_group * tile
            kept = []
            for at in range(0, tile, FOLD):
                key_label = labels_s[start + at : start + at + FOLD, :]
                allowed = jnp.concatenate([key_label, key_label], axis=1) == query_label
                if key_group == query_group:
                    key_at = key_position[at : at + FOLD, :]
                    allowed = allowed & (jnp.concatenate([key_at, key_at], axis=1) <= query_position)
                kept.append(jnp.where(allowed, raw[at : at + FOLD, :], MASKED_SCORE))
                highest = jnp.maximum(highest, kept[-1])
            scores.append(kept)
        return scores, jnp.max(highest, axis=0, keepdims=True)

    def gradient_stage(head, query_group, scores, row_max):
        own = tile_of(head, query_group)
        q_rows, g_rows = q_s[own, :], g_s[own, :]
        total = jnp.zeros((FOLD, tile), jnp.float32)
        weighted = jnp.zeros((FOLD, tile), jnp.float32)
        weights, grads = [], []
        for key_group in range(query_group + 1):
            prob_grad = dot_last(v_s[tile_of(head, key_group), :], g_rows)
            kept, split = [], []
            for index, at in enumerate(range(0, tile, FOLD)):
                weight = jnp.exp2((scores[key_group][index] - row_max) * (scale * LOG2_E))
                grad = prob_grad[at : at + FOLD, :]
                total = total + weight
                weighted = weighted + weight * grad
                kept.append(weight)
                split.append(grad)
            weights.append(kept)
            grads.append(split)
        inverse = 1.0 / jnp.maximum(jnp.sum(total, axis=0, keepdims=True), 1.0)
        delta = jnp.sum(weighted, axis=0, keepdims=True) * inverse
        query_grad = jnp.zeros((LANES, tile), jnp.float32)
        for key_group in range(query_group + 1):
            keys = tile_of(head, key_group)
            probs, score_grads = [], []
            for index in range(0, tile // FOLD, 2):
                pair = []
                for part in (index, index + 1):
                    prob = weights[key_group][part] * inverse
                    pair.append((prob, prob * (grads[key_group][part] - delta)))
                probs.append(jnp.concatenate([pair[0][0], pair[1][0]], axis=0).astype(jnp.bfloat16))
                score_grads.append(jnp.concatenate([pair[0][1], pair[1][1]], axis=0).astype(jnp.bfloat16))
            prob = jnp.concatenate(probs, axis=0)
            score_grad = jnp.concatenate(score_grads, axis=0)
            value_part = dot(prob, g_rows)
            key_part = dot(score_grad, q_rows)
            if key_group == query_group:
                dv_s[keys, :] = value_part
                dk_s[keys, :] = key_part
            else:
                dv_s[keys, :] += value_part
                dk_s[keys, :] += key_part
            query_grad = query_grad + lax.dot_general(
                k_s[keys, :],
                score_grad,
                (((0,), (0,)), ((), ())),
                preferred_element_type=jnp.float32,
            )
        query_rows = jnp.transpose(query_grad) * scale
        for slot in range(SLOTS):
            row = query_group * LANES * back + head * 3 * SLOTS + slot
            back_ref[pl.ds(row, LANES, stride=back), :] = query_rows[slot * LANES : (slot + 1) * LANES, :]

    units = [(head, group) for group in range(groups) for head in range(per_dest)]
    ahead = score_stage(*units[0])
    for index, unit in enumerate(units):
        scores, row_max = ahead
        if index + 1 < len(units):
            ahead = score_stage(*units[index + 1])
        gradient_stage(*unit, scores, row_max)
    for head in range(per_dest):
        for array, grad, factor in ((1, dk_s, scale), (2, dv_s, 1.0)):
            for group in range(groups):
                for slot in range(SLOTS):
                    row = group * LANES * back + (head * 3 + array) * SLOTS + slot
                    at = head * slots + (group * SLOTS + slot) * LANES
                    back_ref[pl.ds(row, LANES, stride=back), :] = grad[at : at + LANES, :] * factor
    out_ref[...] = back_ref[...].astype(jnp.bfloat16)


def unplace_kernel(
    owners, spills, y_ref, select_ref, dq_hbm, dk_hbm, dv_hbm, rows_ref, dq_ref, dk_ref, dv_ref, sems
):
    tokens = dq_ref.shape[0]
    heads = select_ref.shape[0] // tokens
    per_dest = heads // spills
    width = per_dest * LANES
    outs = (dq_ref, dk_ref, dv_ref)
    back = per_dest * len(outs) * SLOTS
    rows_ref[...] = y_ref[...].astype(jnp.float32)
    copies = []
    for head in range(heads):
        dest, within = divmod(head, per_dest)
        stacked = []
        for array in range(len(outs)):
            slots = []
            for slot in range(SLOTS):
                row = (within * len(outs) + array) * SLOTS + slot
                for run in range(owners // RUN):
                    slots.append(rows_ref[run_rows(spills, back, run, dest, row), :])
            stacked.append(jnp.concatenate(slots, axis=0).astype(jnp.bfloat16))
        select = select_ref[head * tokens : (head + 1) * tokens, :]
        result = dot(select, jnp.concatenate(stacked, axis=1)).astype(jnp.bfloat16)
        for array, ref in enumerate(outs):
            ref[:, head * LANES : (head + 1) * LANES] = result[:, array * LANES : (array + 1) * LANES]
        if within == per_dest - 1:
            columns = slice(dest * width, (dest + 1) * width)
            for array, (source, target) in enumerate(zip(outs, (dq_hbm, dk_hbm, dv_hbm))):
                copies.append(
                    pltpu.make_async_copy(
                        source.at[:, columns], target.at[:, columns], sems.at[dest * len(outs) + array]
                    )
                )
                copies[-1].start()
    for copy in copies:
        copy.wait()


def local_ops(owners, spills, tokens, heads):
    devices = owners * spills
    per_dest = heads // spills
    message = per_dest * 4 * SLOTS + SLOTS
    back = per_dest * 3 * SLOTS
    slots = devices * SLOTS
    width = heads * LANES
    whole = pl.BlockSpec(memory_space=pltpu.VMEM)
    hbm = pl.BlockSpec(memory_space=pltpu.HBM)
    params = pltpu.CompilerParams(vmem_limit_bytes=48 * 1024 * 1024)
    token_rows = pltpu.VMEM((tokens, width), jnp.bfloat16)
    grad_shape = jax.ShapeDtypeStruct((tokens, width), jnp.bfloat16)
    place = pl.pallas_call(
        functools.partial(place_kernel, owners, spills),
        out_shape=(
            jax.ShapeDtypeStruct((devices * message, LANES), jnp.bfloat16),
            jax.ShapeDtypeStruct((heads * tokens, SLOTS * owners), jnp.bfloat16),
        ),
        in_specs=[hbm] * 5,
        out_specs=(whole, whole),
        scratch_shapes=[token_rows] * 4
        + [
            pltpu.VMEM((heads, tokens), jnp.int32),
            pltpu.VMEM((heads * SLOTS * owners, tokens), jnp.bfloat16),
            pltpu.VMEM((devices * message, LANES), jnp.float32),
            pltpu.SemaphoreType.DMA((4 * spills + 1,)),
        ],
        compiler_params=params,
        name="place",
    )
    attend = pl.pallas_call(
        functools.partial(attend_kernel, spills, per_dest, message),
        out_shape=jax.ShapeDtypeStruct((devices * back, LANES), jnp.bfloat16),
        in_specs=[whole],
        out_specs=whole,
        scratch_shapes=[
            pltpu.VMEM((devices * message, LANES), jnp.float32),
            pltpu.VMEM((devices * back, LANES), jnp.float32),
            pltpu.VMEM((per_dest * slots, LANES), jnp.bfloat16),
            pltpu.VMEM((per_dest * slots, LANES), jnp.bfloat16),
            pltpu.VMEM((per_dest * slots, LANES), jnp.bfloat16),
            pltpu.VMEM((per_dest * slots, LANES), jnp.bfloat16),
            pltpu.VMEM((per_dest * slots, LANES), jnp.float32),
            pltpu.VMEM((per_dest * slots, LANES), jnp.float32),
            pltpu.VMEM((per_dest * slots, LANES), jnp.float32),
        ],
        compiler_params=params,
        name="attend",
    )
    unplace = pl.pallas_call(
        functools.partial(unplace_kernel, owners, spills),
        out_shape=(grad_shape, grad_shape, grad_shape),
        in_specs=[whole] * 2,
        out_specs=(hbm, hbm, hbm),
        scratch_shapes=[pltpu.VMEM((devices * back, LANES), jnp.float32)]
        + [token_rows] * 3
        + [pltpu.SemaphoreType.DMA((3 * spills,))],
        compiler_params=params,
        name="unplace",
    )
    return place, attend, unplace


def local(queries, keys, values, out_grad, cluster_ids):
    owners, spills = lax.axis_size("outer") * RUN, lax.axis_size("spill")
    devices = owners * spills
    place, attend, unplace = local_ops(owners, spills, *cluster_ids.shape)

    def exchange(rows):
        cut = rows.reshape(devices, -1, SLOTS, LANES)
        moved = lax.all_to_all(cut, ROUTE, split_axis=0, concat_axis=0, tiled=True)
        return moved.reshape(rows.shape)

    inputs = (queries, keys, values, out_grad, jnp.transpose(cluster_ids))
    rows, select = place(*(pltpu.with_memory_space_constraint(x, pltpu.HBM) for x in inputs))
    return unplace(exchange(attend(exchange(rows))), select)


def solution(mesh):
    cut = mesh.devices.reshape(-1, RUN, mesh.shape["spill"])
    mesh = jax.sharding.Mesh(cut, AXES)
    rows = P(AXES, None)
    return jax.shard_map(
        local,
        mesh=mesh,
        in_specs=(rows, rows, rows, rows, rows),
        out_specs=(rows, rows, rows),
        check_vma=False,
    )
```

```python
import functools
import math

import jax
import jax.numpy as jnp
from jax import lax
from jax.experimental import pallas as pl
from jax.experimental.pallas import tpu as pltpu
from jax.sharding import PartitionSpec as P

AXES = ("seq", "spill")
LANES = 128
SLOTS = 2
FOLD = 8
MASKED_SCORE = -1e30
LOWEST_MAX = -5e29
LOG2_E = math.log2(math.e)


def dot(left, right):
    return jnp.dot(left, right, preferred_element_type=jnp.float32)


def dot_last(left, right):
    return lax.dot_general(
        left, right, (((1,), (1,)), ((), ())), preferred_element_type=jnp.float32
    )


def iota(rows, columns, axis):
    return lax.broadcasted_iota(jnp.int32, (rows, columns), axis)


def one_hot_pair(hot, count, axis):
    first = jnp.where(hot & (count < 0.5), 1.0, 0.0)
    second = jnp.where(hot & (count > 0.5), 1.0, 0.0)
    return first, second, jnp.concatenate([first, second], axis=axis).astype(jnp.bfloat16)


def place_kernel(
    owners,
    spills,
    q_hbm,
    k_hbm,
    v_hbm,
    g_hbm,
    ids_hbm,
    out_ref,
    return_ref,
    q_ref,
    k_ref,
    v_ref,
    g_ref,
    ids_ref,
    select_ref,
    rows_ref,
    sems,
):
    heads, tokens = ids_ref.shape
    per_dest = heads // spills
    width = per_dest * LANES
    arrays = (q_ref, k_ref, v_ref, g_ref)
    ids_copy = pltpu.make_async_copy(ids_hbm, ids_ref, sems.at[len(arrays) * spills])
    ids_copy.start()
    copies = []
    for dest in range(spills):
        columns = slice(dest * width, (dest + 1) * width)
        for array, (source, target) in enumerate(zip((q_hbm, k_hbm, v_hbm, g_hbm), arrays)):
            copies.append(
                pltpu.make_async_copy(
                    source.at[:, columns], target.at[:, columns], sems.at[dest * len(arrays) + array]
                )
            )
            copies[-1].start()
    data_rows = per_dest * len(arrays) * SLOTS
    message = data_rows + SLOTS
    pitch = spills * message + 1
    token_before = iota(tokens, tokens, 0) < iota(tokens, tokens, 1)
    before = jnp.where(token_before, 1.0, 0.0).astype(jnp.bfloat16)
    after = jnp.where(iota(tokens, tokens, 1) < iota(tokens, tokens, 0), 1.0, 0.0).astype(jnp.bfloat16)
    half_lanes = iota(owners, LANES, 1) // (LANES // per_dest)
    ids_copy.wait()
    ids = ids_ref[...]
    all_owners = ids % owners
    all_labels = (ids // owners + 1).astype(jnp.float32)
    owner_columns = jnp.transpose(all_owners.astype(jnp.float32)).astype(jnp.int32)
    for dest in range(spills):
        slot_labels = [jnp.zeros((owners, LANES), jnp.float32)] * SLOTS
        for within in range(per_dest):
            head = dest * per_dest + within
            hot = all_owners[head : head + 1, :] == iota(owners, tokens, 0)
            count = dot(jnp.where(hot, 1.0, 0.0).astype(jnp.bfloat16), before)
            first, second, select = one_hot_pair(hot, count, 0)
            select_ref[head * SLOTS * owners : (head + 1) * SLOTS * owners, :] = select
            label = all_labels[head : head + 1, :]
            for slot, mask in enumerate((first, second)):
                slot_label = jnp.sum(mask * label, axis=1, keepdims=True)
                slot_labels[slot] = jnp.where(half_lanes == within, slot_label, slot_labels[slot])
            hot = owner_columns[:, head : head + 1] == iota(tokens, owners, 1)
            count = dot(after, jnp.where(hot, 1.0, 0.0).astype(jnp.bfloat16))
            return_ref[head * tokens : (head + 1) * tokens, :] = one_hot_pair(hot, count, 1)[2]
        for slot in range(SLOTS):
            row = dest * message + data_rows + slot
            rows_ref[pl.ds(row, owners, stride=pitch), :] = slot_labels[slot]
    for head in range(heads):
        dest, within = divmod(head, per_dest)
        if within == 0:
            for copy in copies[dest * len(arrays) : (dest + 1) * len(arrays)]:
                copy.wait()
        columns = slice(head * LANES, (head + 1) * LANES)
        placed = dot(
            select_ref[head * SLOTS * owners : (head + 1) * SLOTS * owners, :],
            jnp.concatenate([ref[:, columns] for ref in arrays], axis=1),
        )
        for array in range(len(arrays)):
            for slot in range(SLOTS):
                row = dest * message + (within * len(arrays) + array) * SLOTS + slot
                rows_ref[pl.ds(row, owners, stride=pitch), :] = placed[
                    slot * owners : (slot + 1) * owners, array * LANES : (array + 1) * LANES
                ]
    for owner in range(0, owners, 2):
        pair = [rows_ref[at * pitch : (at + 1) * pitch - 1, :] for at in (owner, owner + 1)]
        out_ref[owner * (pitch - 1) : (owner + 2) * (pitch - 1), :] = jnp.concatenate(pair, axis=0).astype(
            jnp.bfloat16
        )


def attend_kernel(
    per_dest, message, x_ref, out_ref, rows_ref, back_ref, q_s, k_s, v_s, g_s, labels_s, dk_s, dv_s
):
    blocks = x_ref.shape[0] // message
    back = out_ref.shape[0] // blocks
    groups = blocks // LANES
    tile = SLOTS * LANES
    slots = blocks * SLOTS
    scale = LANES ** (-0.5)
    arrays = (q_s, k_s, v_s, g_s)
    rows_ref[: x_ref.shape[0], :] = x_ref[...].astype(jnp.float32)
    key_at = SLOTS * (iota(tile, tile, 0) % LANES) + iota(tile, tile, 0) // LANES
    query_at = SLOTS * (iota(tile, tile, 1) % LANES) + iota(tile, tile, 1) // LANES
    causal = key_at <= query_at
    query_labels = [[None] * groups for _ in range(per_dest)]
    for group in range(groups):
        first_row = group * LANES * message
        for slot in range(SLOTS):
            at = (group * SLOTS + slot) * LANES
            for head in range(per_dest):
                for array, scratch in enumerate(arrays):
                    row = first_row + (head * len(arrays) + array) * SLOTS + slot
                    scratch[head * slots + at : head * slots + at + LANES, :] = rows_ref[
                        pl.ds(row, LANES, stride=message), :
                    ].astype(jnp.bfloat16)
            row = first_row + per_dest * len(arrays) * SLOTS + slot
            label = rows_ref[pl.ds(row, LANES, stride=message), :]
            turned = jnp.transpose(label)
            for head in range(per_dest):
                lane = head * (LANES // per_dest)
                labels_s[head * slots + at : head * slots + at + LANES, :] = jnp.broadcast_to(
                    label[:, lane : lane + 1], (LANES, LANES)
                )
                part = turned[lane : lane + 1, :]
                part = jnp.where(part > 0.5, part, -1.0)
                before = query_labels[head][group]
                query_labels[head][group] = part if slot == 0 else jnp.concatenate([before, part], axis=1)

    def tile_of(head, group):
        start = head * slots + group * tile
        return slice(start, start + tile)

    def score_stage(head, query_group):
        q_rows = q_s[tile_of(head, query_group), :]
        query_label = query_labels[head][query_group]
        scores = []
        highest = jnp.full((FOLD, tile), LOWEST_MAX, jnp.float32)
        for key_group in range(query_group + 1):
            raw = dot_last(k_s[tile_of(head, key_group), :], q_rows)
            start = head * slots + key_group * tile
            kept = []
            for at in range(0, tile, FOLD):
                key_label = labels_s[start + at : start + at + FOLD, :]
                allowed = jnp.concatenate([key_label, key_label], axis=1) == query_label
                if key_group == query_group:
                    allowed = allowed & causal[at : at + FOLD, :]
                kept.append(jnp.where(allowed, raw[at : at + FOLD, :], MASKED_SCORE))
                highest = jnp.maximum(highest, kept[-1])
            scores.append(kept)
        return scores, jnp.max(highest, axis=0, keepdims=True)

    def gradient_stage(head, query_group, scores, row_max):
        own = tile_of(head, query_group)
        q_rows, g_rows = q_s[own, :], g_s[own, :]
        total = jnp.zeros((FOLD, tile), jnp.float32)
        weighted = jnp.zeros((FOLD, tile), jnp.float32)
        weights, grads = [], []
        for key_group in range(query_group + 1):
            prob_grad = dot_last(v_s[tile_of(head, key_group), :], g_rows)
            kept, split = [], []
            for index, at in enumerate(range(0, tile, FOLD)):
                weight = jnp.exp2((scores[key_group][index] - row_max) * (scale * LOG2_E))
                grad = prob_grad[at : at + FOLD, :]
                total = total + weight
                weighted = weighted + weight * grad
                kept.append(weight)
                split.append(grad)
            weights.append(kept)
            grads.append(split)
        inverse = 1.0 / jnp.maximum(jnp.sum(total, axis=0, keepdims=True), 1.0)
        delta = jnp.sum(weighted, axis=0, keepdims=True) * inverse
        query_grad = jnp.zeros((LANES, tile), jnp.float32)
        for key_group in range(query_group + 1):
            keys = tile_of(head, key_group)
            probs, score_grads = [], []
            for index in range(0, tile // FOLD, 2):
                pair = []
                for part in (index, index + 1):
                    prob = weights[key_group][part] * inverse
                    pair.append((prob, prob * (grads[key_group][part] - delta)))
                probs.append(jnp.concatenate([pair[0][0], pair[1][0]], axis=0).astype(jnp.bfloat16))
                score_grads.append(jnp.concatenate([pair[0][1], pair[1][1]], axis=0).astype(jnp.bfloat16))
            prob = jnp.concatenate(probs, axis=0)
            score_grad = jnp.concatenate(score_grads, axis=0)
            value_part = dot(prob, g_rows)
            key_part = dot(score_grad, q_rows)
            if key_group == query_group:
                dv_s[keys, :] = value_part
                dk_s[keys, :] = key_part
            else:
                dv_s[keys, :] += value_part
                dk_s[keys, :] += key_part
            query_grad = query_grad + lax.dot_general(
                k_s[keys, :],
                score_grad,
                (((0,), (0,)), ((), ())),
                preferred_element_type=jnp.float32,
            )
        query_rows = jnp.transpose(query_grad) * scale
        for slot in range(SLOTS):
            row = query_group * LANES * back + head * 3 * SLOTS + slot
            back_ref[pl.ds(row, LANES, stride=back), :] = query_rows[slot * LANES : (slot + 1) * LANES, :]

    units = [(head, group) for group in range(groups) for head in range(per_dest)]
    ahead = score_stage(*units[0])
    for index, unit in enumerate(units):
        scores, row_max = ahead
        if index + 1 < len(units):
            ahead = score_stage(*units[index + 1])
        gradient_stage(*unit, scores, row_max)
    for head in range(per_dest):
        for array, grad, factor in ((1, dk_s, scale), (2, dv_s, 1.0)):
            for group in range(groups):
                for slot in range(SLOTS):
                    row = group * LANES * back + (head * 3 + array) * SLOTS + slot
                    at = head * slots + (group * SLOTS + slot) * LANES
                    back_ref[pl.ds(row, LANES, stride=back), :] = grad[at : at + LANES, :] * factor
    out_ref[...] = back_ref[: out_ref.shape[0], :].astype(jnp.bfloat16)


def unplace_kernel(
    owners, spills, y_ref, select_ref, dq_hbm, dk_hbm, dv_hbm, rows_ref, dq_ref, dk_ref, dv_ref, sems
):
    tokens = dq_ref.shape[0]
    heads = select_ref.shape[0] // tokens
    per_dest = heads // spills
    width = per_dest * LANES
    outs = (dq_ref, dk_ref, dv_ref)
    back = per_dest * len(outs) * SLOTS
    pitch = spills * back + 1
    for owner in range(owners):
        rows_ref[owner * pitch : (owner + 1) * pitch - 1, :] = y_ref[
            owner * (pitch - 1) : (owner + 1) * (pitch - 1), :
        ].astype(jnp.float32)
    copies = []
    for head in range(heads):
        dest, within = divmod(head, per_dest)
        stacked = []
        for array in range(len(outs)):
            slots = []
            for slot in range(SLOTS):
                row = dest * back + (within * len(outs) + array) * SLOTS + slot
                slots.append(rows_ref[pl.ds(row, owners, stride=pitch), :])
            stacked.append(jnp.concatenate(slots, axis=0).astype(jnp.bfloat16))
        select = select_ref[head * tokens : (head + 1) * tokens, :]
        result = dot(select, jnp.concatenate(stacked, axis=1)).astype(jnp.bfloat16)
        for array, ref in enumerate(outs):
            ref[:, head * LANES : (head + 1) * LANES] = result[:, array * LANES : (array + 1) * LANES]
        if within == per_dest - 1:
            columns = slice(dest * width, (dest + 1) * width)
            for array, (source, target) in enumerate(zip(outs, (dq_hbm, dk_hbm, dv_hbm))):
                copies.append(
                    pltpu.make_async_copy(
                        source.at[:, columns], target.at[:, columns], sems.at[dest * len(outs) + array]
                    )
                )
                copies[-1].start()
    for copy in copies:
        copy.wait()


def strided_rows(count, pitch):
    return pltpu.VMEM((-(-(count + 1) * pitch // FOLD) * FOLD, LANES), jnp.float32)


def local_ops(owners, spills, tokens, heads):
    devices = owners * spills
    per_dest = heads // spills
    message = per_dest * 4 * SLOTS + SLOTS
    back = per_dest * 3 * SLOTS
    slots = devices * SLOTS
    width = heads * LANES
    whole = pl.BlockSpec(memory_space=pltpu.VMEM)
    hbm = pl.BlockSpec(memory_space=pltpu.HBM)
    params = pltpu.CompilerParams(vmem_limit_bytes=48 * 1024 * 1024)
    token_rows = pltpu.VMEM((tokens, width), jnp.bfloat16)
    grad_shape = jax.ShapeDtypeStruct((tokens, width), jnp.bfloat16)
    place = pl.pallas_call(
        functools.partial(place_kernel, owners, spills),
        out_shape=(
            jax.ShapeDtypeStruct((devices * message, LANES), jnp.bfloat16),
            jax.ShapeDtypeStruct((heads * tokens, SLOTS * owners), jnp.bfloat16),
        ),
        in_specs=[hbm] * 5,
        out_specs=(whole, whole),
        scratch_shapes=[token_rows] * 4
        + [
            pltpu.VMEM((heads, tokens), jnp.int32),
            pltpu.VMEM((heads * SLOTS * owners, tokens), jnp.bfloat16),
            strided_rows(owners, spills * message + 1),
            pltpu.SemaphoreType.DMA((4 * spills + 1,)),
        ],
        compiler_params=params,
        name="place",
    )
    attend = pl.pallas_call(
        functools.partial(attend_kernel, per_dest, message),
        out_shape=jax.ShapeDtypeStruct((devices * back, LANES), jnp.bfloat16),
        in_specs=[whole],
        out_specs=whole,
        scratch_shapes=[
            strided_rows(devices, message),
            strided_rows(devices, back),
            pltpu.VMEM((per_dest * slots, LANES), jnp.bfloat16),
            pltpu.VMEM((per_dest * slots, LANES), jnp.bfloat16),
            pltpu.VMEM((per_dest * slots, LANES), jnp.bfloat16),
            pltpu.VMEM((per_dest * slots, LANES), jnp.bfloat16),
            pltpu.VMEM((per_dest * slots, LANES), jnp.float32),
            pltpu.VMEM((per_dest * slots, LANES), jnp.float32),
            pltpu.VMEM((per_dest * slots, LANES), jnp.float32),
        ],
        compiler_params=params,
        name="attend",
    )
    unplace = pl.pallas_call(
        functools.partial(unplace_kernel, owners, spills),
        out_shape=(grad_shape, grad_shape, grad_shape),
        in_specs=[whole] * 2,
        out_specs=(hbm, hbm, hbm),
        scratch_shapes=[strided_rows(owners, spills * back + 1)]
        + [token_rows] * 3
        + [pltpu.SemaphoreType.DMA((3 * spills,))],
        compiler_params=params,
        name="unplace",
    )
    return place, attend, unplace


def local(queries, keys, values, out_grad, cluster_ids):
    owners, spills = lax.axis_size("seq"), lax.axis_size("spill")
    devices = owners * spills
    place, attend, unplace = local_ops(owners, spills, *cluster_ids.shape)

    def exchange(rows):
        cut = rows.reshape(devices, -1, SLOTS, LANES)
        moved = lax.all_to_all(cut, AXES, split_axis=0, concat_axis=0, tiled=True)
        return moved.reshape(rows.shape)

    inputs = (queries, keys, values, out_grad, jnp.transpose(cluster_ids))
    rows, select = place(*(pltpu.with_memory_space_constraint(x, pltpu.HBM) for x in inputs))
    return unplace(exchange(attend(exchange(rows))), select)


def solution(mesh):
    rows = P(AXES, None)
    return jax.shard_map(
        local,
        mesh=mesh,
        in_specs=(rows, rows, rows, rows, rows),
        out_specs=(rows, rows, rows),
        check_vma=False,
    )
```

```python
import functools
import math

import jax
import jax.numpy as jnp
from jax import lax
from jax.experimental import pallas as pl
from jax.experimental.pallas import tpu as pltpu
from jax.sharding import PartitionSpec as P

AXES = ("seq", "spill")
LANES = 128
SLOTS = 2
FOLD = 8
MASKED_SCORE = -1e30
LOWEST_MAX = -5e29
LOG2_E = math.log2(math.e)


def dot(left, right):
    return jnp.dot(left, right, preferred_element_type=jnp.float32)


def dot_last(left, right):
    return lax.dot_general(
        left, right, (((1,), (1,)), ((), ())), preferred_element_type=jnp.float32
    )


def iota(rows, columns, axis):
    return lax.broadcasted_iota(jnp.int32, (rows, columns), axis)


def one_hot_pair(hot, count, axis):
    first = jnp.where(hot & (count < 0.5), 1.0, 0.0)
    second = jnp.where(hot & (count > 0.5), 1.0, 0.0)
    return first, second, jnp.concatenate([first, second], axis=axis).astype(jnp.bfloat16)


def place_kernel(
    owners,
    spills,
    q_hbm,
    k_hbm,
    v_hbm,
    g_hbm,
    ids_hbm,
    out_ref,
    return_ref,
    q_ref,
    k_ref,
    v_ref,
    g_ref,
    ids_ref,
    select_ref,
    rows_ref,
    sems,
):
    heads, tokens = ids_ref.shape
    per_dest = heads // spills
    arrays = (q_ref, k_ref, v_ref, g_ref)
    ids_copy = pltpu.make_async_copy(ids_hbm, ids_ref, sems.at[len(arrays)])
    ids_copy.start()
    copies = []
    for array, (source, target) in enumerate(zip((q_hbm, k_hbm, v_hbm, g_hbm), arrays)):
        copies.append(pltpu.make_async_copy(source, target, sems.at[array]))
        copies[-1].start()
    data_rows = per_dest * len(arrays) * SLOTS
    message = data_rows + SLOTS
    pitch = spills * message + 1
    token_before = iota(tokens, tokens, 0) < iota(tokens, tokens, 1)
    before = jnp.where(token_before, 1.0, 0.0).astype(jnp.bfloat16)
    after = jnp.where(iota(tokens, tokens, 1) < iota(tokens, tokens, 0), 1.0, 0.0).astype(jnp.bfloat16)
    half_lanes = iota(owners, LANES, 1) // (LANES // per_dest)
    ids_copy.wait()
    ids = ids_ref[...]
    all_owners = ids % owners
    all_labels = (ids // owners + 1).astype(jnp.float32)
    owner_columns = jnp.transpose(all_owners.astype(jnp.float32)).astype(jnp.int32)

    def choose(dest):
        slot_labels = [jnp.zeros((owners, LANES), jnp.float32)] * SLOTS
        for within in range(per_dest):
            head = dest * per_dest + within
            hot = all_owners[head : head + 1, :] == iota(owners, tokens, 0)
            count = dot(jnp.where(hot, 1.0, 0.0).astype(jnp.bfloat16), before)
            first, second, select = one_hot_pair(hot, count, 0)
            select_ref[head * SLOTS * owners : (head + 1) * SLOTS * owners, :] = select
            label = all_labels[head : head + 1, :]
            for slot, mask in enumerate((first, second)):
                slot_label = jnp.sum(mask * label, axis=1, keepdims=True)
                slot_labels[slot] = jnp.where(half_lanes == within, slot_label, slot_labels[slot])
        for slot in range(SLOTS):
            row = dest * message + data_rows + slot
            rows_ref[pl.ds(row, owners, stride=pitch), :] = slot_labels[slot]

    def choose_return(dest):
        for head in range(dest * per_dest, (dest + 1) * per_dest):
            hot = owner_columns[:, head : head + 1] == iota(tokens, owners, 1)
            count = dot(after, jnp.where(hot, 1.0, 0.0).astype(jnp.bfloat16))
            return_ref[head * tokens : (head + 1) * tokens, :] = one_hot_pair(hot, count, 1)[2]

    for dest in range(spills):
        choose(dest)
    for copy in copies:
        copy.wait()
    for dest in range(spills):
        for within in range(per_dest):
            head = dest * per_dest + within
            columns = slice(head * LANES, (head + 1) * LANES)
            placed = dot(
                select_ref[head * SLOTS * owners : (head + 1) * SLOTS * owners, :],
                jnp.concatenate([ref[:, columns] for ref in arrays], axis=1),
            )
            for array in range(len(arrays)):
                for slot in range(SLOTS):
                    row = dest * message + (within * len(arrays) + array) * SLOTS + slot
                    rows_ref[pl.ds(row, owners, stride=pitch), :] = placed[
                        slot * owners : (slot + 1) * owners, array * LANES : (array + 1) * LANES
                    ]
        choose_return(dest)
    for owner in range(0, owners, 2):
        pair = [rows_ref[at * pitch : (at + 1) * pitch - 1, :] for at in (owner, owner + 1)]
        out_ref[owner * (pitch - 1) : (owner + 2) * (pitch - 1), :] = jnp.concatenate(pair, axis=0).astype(
            jnp.bfloat16
        )


def attend_kernel(
    per_dest, message, x_ref, out_ref, rows_ref, back_ref, q_s, k_s, v_s, g_s, labels_s, dk_s, dv_s
):
    blocks = x_ref.shape[0] // message
    back = out_ref.shape[0] // blocks
    groups = blocks // LANES
    tile = SLOTS * LANES
    slots = blocks * SLOTS
    scale = LANES ** (-0.5)
    arrays = (q_s, k_s, v_s, g_s)
    rows_ref[: x_ref.shape[0], :] = x_ref[...].astype(jnp.float32)
    key_at = SLOTS * (iota(tile, tile, 0) % LANES) + iota(tile, tile, 0) // LANES
    query_at = SLOTS * (iota(tile, tile, 1) % LANES) + iota(tile, tile, 1) // LANES
    causal = key_at <= query_at
    query_labels = [[None] * groups for _ in range(per_dest)]
    for group in range(groups):
        first_row = group * LANES * message
        for slot in range(SLOTS):
            at = (group * SLOTS + slot) * LANES
            for head in range(per_dest):
                for array, scratch in enumerate(arrays):
                    row = first_row + (head * len(arrays) + array) * SLOTS + slot
                    scratch[head * slots + at : head * slots + at + LANES, :] = rows_ref[
                        pl.ds(row, LANES, stride=message), :
                    ].astype(jnp.bfloat16)
            row = first_row + per_dest * len(arrays) * SLOTS + slot
            label = rows_ref[pl.ds(row, LANES, stride=message), :]
            turned = jnp.transpose(label)
            for head in range(per_dest):
                lane = head * (LANES // per_dest)
                labels_s[head * slots + at : head * slots + at + LANES, :] = jnp.broadcast_to(
                    label[:, lane : lane + 1], (LANES, LANES)
                )
                part = turned[lane : lane + 1, :]
                part = jnp.where(part > 0.5, part, -1.0)
                before = query_labels[head][group]
                query_labels[head][group] = part if slot == 0 else jnp.concatenate([before, part], axis=1)

    def tile_of(head, group):
        start = head * slots + group * tile
        return slice(start, start + tile)

    def score_stage(head, query_group):
        q_rows = q_s[tile_of(head, query_group), :]
        query_label = query_labels[head][query_group]
        scores = []
        highest = jnp.full((FOLD, tile), LOWEST_MAX, jnp.float32)
        for key_group in range(query_group + 1):
            raw = dot_last(k_s[tile_of(head, key_group), :], q_rows)
            start = head * slots + key_group * tile
            kept = []
            for at in range(0, tile, FOLD):
                key_label = labels_s[start + at : start + at + FOLD, :]
                allowed = jnp.concatenate([key_label, key_label], axis=1) == query_label
                if key_group == query_group:
                    allowed = allowed & causal[at : at + FOLD, :]
                kept.append(jnp.where(allowed, raw[at : at + FOLD, :], MASKED_SCORE))
                highest = jnp.maximum(highest, kept[-1])
            scores.append(kept)
        return scores, jnp.max(highest, axis=0, keepdims=True)

    def gradient_stage(head, query_group, scores, row_max):
        own = tile_of(head, query_group)
        q_rows, g_rows = q_s[own, :], g_s[own, :]
        total = jnp.zeros((FOLD, tile), jnp.float32)
        weighted = jnp.zeros((FOLD, tile), jnp.float32)
        weights, grads = [], []
        for key_group in range(query_group + 1):
            prob_grad = dot_last(v_s[tile_of(head, key_group), :], g_rows)
            kept, split = [], []
            for index, at in enumerate(range(0, tile, FOLD)):
                weight = jnp.exp2((scores[key_group][index] - row_max) * (scale * LOG2_E))
                grad = prob_grad[at : at + FOLD, :]
                total = total + weight
                weighted = weighted + weight * grad
                kept.append(weight)
                split.append(grad)
            weights.append(kept)
            grads.append(split)
        inverse = 1.0 / jnp.maximum(jnp.sum(total, axis=0, keepdims=True), 1.0)
        delta = jnp.sum(weighted, axis=0, keepdims=True) * inverse
        query_grad = jnp.zeros((LANES, tile), jnp.float32)
        for key_group in range(query_group + 1):
            keys = tile_of(head, key_group)
            probs, score_grads = [], []
            for index in range(0, tile // FOLD, 2):
                pair = []
                for part in (index, index + 1):
                    prob = weights[key_group][part] * inverse
                    pair.append((prob, prob * (grads[key_group][part] - delta)))
                probs.append(jnp.concatenate([pair[0][0], pair[1][0]], axis=0).astype(jnp.bfloat16))
                score_grads.append(jnp.concatenate([pair[0][1], pair[1][1]], axis=0).astype(jnp.bfloat16))
            prob = jnp.concatenate(probs, axis=0)
            score_grad = jnp.concatenate(score_grads, axis=0)
            value_part = dot(prob, g_rows)
            key_part = dot(score_grad, q_rows)
            if key_group == query_group:
                dv_s[keys, :] = value_part
                dk_s[keys, :] = key_part
            else:
                dv_s[keys, :] += value_part
                dk_s[keys, :] += key_part
            query_grad = query_grad + lax.dot_general(
                k_s[keys, :],
                score_grad,
                (((0,), (0,)), ((), ())),
                preferred_element_type=jnp.float32,
            )
        query_rows = jnp.transpose(query_grad) * scale
        for slot in range(SLOTS):
            row = query_group * LANES * back + head * 3 * SLOTS + slot
            back_ref[pl.ds(row, LANES, stride=back), :] = query_rows[slot * LANES : (slot + 1) * LANES, :]

    units = [(head, group) for group in range(groups) for head in range(per_dest)]
    ahead = score_stage(*units[0])
    for index, unit in enumerate(units):
        scores, row_max = ahead
        if index + 1 < len(units):
            ahead = score_stage(*units[index + 1])
        gradient_stage(*unit, scores, row_max)
    for head in range(per_dest):
        for array, grad, factor in ((1, dk_s, scale), (2, dv_s, 1.0)):
            for group in range(groups):
                for slot in range(SLOTS):
                    row = group * LANES * back + (head * 3 + array) * SLOTS + slot
                    at = head * slots + (group * SLOTS + slot) * LANES
                    back_ref[pl.ds(row, LANES, stride=back), :] = grad[at : at + LANES, :] * factor
    out_ref[...] = back_ref[: out_ref.shape[0], :].astype(jnp.bfloat16)


def unplace_kernel(
    owners, spills, y_ref, select_ref, dq_hbm, dk_hbm, dv_hbm, rows_ref, dq_ref, dk_ref, dv_ref, sems
):
    tokens = dq_ref.shape[0]
    heads = select_ref.shape[0] // tokens
    per_dest = heads // spills
    width = per_dest * LANES
    outs = (dq_ref, dk_ref, dv_ref)
    back = per_dest * len(outs) * SLOTS
    pitch = spills * back + 1
    for owner in range(owners):
        rows_ref[owner * pitch : (owner + 1) * pitch - 1, :] = y_ref[
            owner * (pitch - 1) : (owner + 1) * (pitch - 1), :
        ].astype(jnp.float32)
    copies = []
    for head in range(heads):
        dest, within = divmod(head, per_dest)
        stacked = []
        for array in range(len(outs)):
            slots = []
            for slot in range(SLOTS):
                row = dest * back + (within * len(outs) + array) * SLOTS + slot
                slots.append(rows_ref[pl.ds(row, owners, stride=pitch), :])
            stacked.append(jnp.concatenate(slots, axis=0).astype(jnp.bfloat16))
        select = select_ref[head * tokens : (head + 1) * tokens, :]
        result = dot(select, jnp.concatenate(stacked, axis=1)).astype(jnp.bfloat16)
        for array, ref in enumerate(outs):
            ref[:, head * LANES : (head + 1) * LANES] = result[:, array * LANES : (array + 1) * LANES]
        if within == per_dest - 1:
            columns = slice(dest * width, (dest + 1) * width)
            for array, (source, target) in enumerate(zip(outs, (dq_hbm, dk_hbm, dv_hbm))):
                copies.append(
                    pltpu.make_async_copy(
                        source.at[:, columns], target.at[:, columns], sems.at[dest * len(outs) + array]
                    )
                )
                copies[-1].start()
    for copy in copies:
        copy.wait()


def strided_rows(count, pitch):
    return pltpu.VMEM((-(-(count + 1) * pitch // FOLD) * FOLD, LANES), jnp.float32)


def local_ops(owners, spills, tokens, heads):
    devices = owners * spills
    per_dest = heads // spills
    message = per_dest * 4 * SLOTS + SLOTS
    back = per_dest * 3 * SLOTS
    slots = devices * SLOTS
    width = heads * LANES
    whole = pl.BlockSpec(memory_space=pltpu.VMEM)
    hbm = pl.BlockSpec(memory_space=pltpu.HBM)
    params = pltpu.CompilerParams(vmem_limit_bytes=48 * 1024 * 1024)
    token_rows = pltpu.VMEM((tokens, width), jnp.bfloat16)
    grad_shape = jax.ShapeDtypeStruct((tokens, width), jnp.bfloat16)
    place = pl.pallas_call(
        functools.partial(place_kernel, owners, spills),
        out_shape=(
            jax.ShapeDtypeStruct((devices * message, LANES), jnp.bfloat16),
            jax.ShapeDtypeStruct((heads * tokens, SLOTS * owners), jnp.bfloat16),
        ),
        in_specs=[hbm] * 5,
        out_specs=(whole, whole),
        scratch_shapes=[token_rows] * 4
        + [
            pltpu.VMEM((heads, tokens), jnp.int32),
            pltpu.VMEM((heads * SLOTS * owners, tokens), jnp.bfloat16),
            strided_rows(owners, spills * message + 1),
            pltpu.SemaphoreType.DMA((5,)),
        ],
        compiler_params=params,
        name="place",
    )
    attend = pl.pallas_call(
        functools.partial(attend_kernel, per_dest, message),
        out_shape=jax.ShapeDtypeStruct((devices * back, LANES), jnp.bfloat16),
        in_specs=[whole],
        out_specs=whole,
        scratch_shapes=[
            strided_rows(devices, message),
            strided_rows(devices, back),
            pltpu.VMEM((per_dest * slots, LANES), jnp.bfloat16),
            pltpu.VMEM((per_dest * slots, LANES), jnp.bfloat16),
            pltpu.VMEM((per_dest * slots, LANES), jnp.bfloat16),
            pltpu.VMEM((per_dest * slots, LANES), jnp.bfloat16),
            pltpu.VMEM((per_dest * slots, LANES), jnp.float32),
            pltpu.VMEM((per_dest * slots, LANES), jnp.float32),
            pltpu.VMEM((per_dest * slots, LANES), jnp.float32),
        ],
        compiler_params=params,
        name="attend",
    )
    unplace = pl.pallas_call(
        functools.partial(unplace_kernel, owners, spills),
        out_shape=(grad_shape, grad_shape, grad_shape),
        in_specs=[whole] * 2,
        out_specs=(hbm, hbm, hbm),
        scratch_shapes=[strided_rows(owners, spills * back + 1)]
        + [token_rows] * 3
        + [pltpu.SemaphoreType.DMA((3 * spills,))],
        compiler_params=params,
        name="unplace",
    )
    return place, attend, unplace


def local(queries, keys, values, out_grad, cluster_ids):
    owners, spills = lax.axis_size("seq"), lax.axis_size("spill")
    devices = owners * spills
    place, attend, unplace = local_ops(owners, spills, *cluster_ids.shape)

    def exchange(rows):
        cut = rows.reshape(devices, -1, SLOTS, LANES)
        moved = lax.all_to_all(cut, AXES, split_axis=0, concat_axis=0, tiled=True)
        return moved.reshape(rows.shape)

    inputs = (queries, keys, values, out_grad, jnp.transpose(cluster_ids))
    rows, select = place(*(pltpu.with_memory_space_constraint(x, pltpu.HBM) for x in inputs))
    return unplace(exchange(attend(exchange(rows))), select)


def solution(mesh):
    rows = P(AXES, None)
    return jax.shard_map(
        local,
        mesh=mesh,
        in_specs=(rows, rows, rows, rows, rows),
        out_specs=(rows, rows, rows),
        check_vma=False,
    )
```
